128 devices in a mesh: pipe: 4 (over z_hi, core), tensor: 4 (over x), dp: 8 (over z_lo, y).
Axes of the slice: x: 4, y: 4, z: 4 (z_hi: 2, z_lo: 2; z = z_hi * 2 + z_lo), core: 2. Of those that a mesh axis runs over, the one named last changes fastest.
Arguments:
- inputs: bfloat16 [2, 512, 4096], P(None, ('tensor', 'dp')), may hold values from -6 to 6
- weights: bfloat16 [2, 4, 4096, 4096], P(None, 'pipe', None, 'tensor'), may hold values from -0.09375 to 0.09375
- norm_gains: float32 [2, 4, 4096], P(None, 'pipe'), may hold values from 0.1 to 1.9
- cotangent: bfloat16 [2, 512, 4096], P(None, ('tensor', 'dp')), may hold values from -6 to 6
Outputs:
- act_factor: bfloat16 [4096, 2, 4, 4096], P(('tensor', 'dp'), None, 'pipe')
- grad_factor: bfloat16 [4096, 2, 4, 4096], P(('tensor', 'dp'), None, 'pipe')
The draws below stay inside these ranges and needn't reach their ends.
All inputs are finite; a program needn't handle non-finite values.
Results may differ from the reference program's by a relative error of at most 0.025.
Values may be sent and summed in bfloat16 or wider, within the bound.
No kernel may reach another device: no remote copies, remote signals or barrier semaphores. Data moves between devices by JAX's collectives and lax.ppermute only.
A program may use at most 192 MiB of HBM per device.

```python
import jax
import jax.numpy as jnp
from jax import lax

D = 4096
MB_DEV = 16
MICRO = 2
SLOTS = 2
LAYERS = 8
MICRO_TOKENS = 512
N_PIPE = 4
N_TENSOR = 4
N_DP = 8


def steps_of(own_key, dims, split, least, largest):
    def one(dim, parts):
        draws = jax.random.uniform(jax.random.fold_in(jax.random.fold_in(own_key, 6), dim), (parts,), jnp.float32, least / len(split), largest / len(split))
        return jnp.repeat(jnp.exp(draws), dims[dim] // parts).reshape((-1,) + (1,) * (len(dims) - dim - 1))

    loudness = one(*split[0])
    for cut in split[1:]:
        loudness = loudness * one(*cut)
    return loudness


def gaussian(key, shape, deviation, bound, split=(), dtype=jnp.bfloat16):
    array = deviation * jax.random.normal(key, shape, jnp.float32)
    if split:
        array = array * steps_of(key, shape, split, -0.22, 0.18)
    return jnp.clip(array, -bound, bound).astype(dtype)


def setup_inputs(seed: int = 0) -> dict:
    key_of = jax.random.split(jax.random.key(seed), 5)
    inputs = gaussian(key_of[0], (MICRO, MICRO_TOKENS, D), 1.0, 6.0, ((1, 32),))
    weights = gaussian(key_of[1], (SLOTS, N_PIPE, D, D), D ** -0.5, 0.09375, ((1, 4), (3, 4)))
    norm_gains = jnp.clip(1.0 + 0.18 * jax.random.normal(key_of[2], (SLOTS, N_PIPE, D), jnp.float32), 0.1, 1.9)
    cotangent = gaussian(key_of[3], (MICRO, MICRO_TOKENS, D), 1.0, 6.0, ((1, 32),))
    return {"inputs": inputs, "weights": weights, "norm_gains": norm_gains, "cotangent": cotangent}


EPSILON = 1e-05

def normalize(hidden, gain_row):
    hidden_wide = hidden.astype(jnp.float32)
    inverse_rms = lax.rsqrt(lax.optimization_barrier(jnp.mean(hidden_wide * hidden_wide, axis=-1, keepdims=True)) + EPSILON)
    normed = (hidden_wide * inverse_rms * gain_row).astype(jnp.bfloat16)
    return (hidden_wide, inverse_rms, normed)

def rounded(values):
    return lax.optimization_barrier(values.astype(jnp.bfloat16)).astype(jnp.float32)

def group_gram(tokens):
    grouped = tokens.reshape(MICRO, N_TENSOR, N_DP, MB_DEV, D)

    def add_group(group_pick, totals):
        chosen = lax.dynamic_index_in_dim(grouped, group_pick, 2, keepdims=False)
        flat_rows = chosen.reshape(MICRO * N_TENSOR * MB_DEV, D)
        gram = lax.dot_general(flat_rows, flat_rows, (((0,), (0,)), ((), ())), preferred_element_type=jnp.float32)
        return totals + rounded(gram * (1.0 / (MICRO * MICRO_TOKENS)))
    totals = lax.fori_loop(0, N_DP, add_group, jnp.zeros((D, D), jnp.float32))
    return totals.astype(jnp.bfloat16)

def reference(inputs, weights, norm_gains, cotangent):
    quarter = D // N_TENSOR
    hidden = inputs
    saved_hidden = []
    act_list = []
    for layer_index in range(LAYERS):
        slot_pick = layer_index // N_PIPE
        section_pick = layer_index % N_PIPE
        hidden_wide, inverse_rms, normed = normalize(hidden, norm_gains[slot_pick, section_pick])
        saved_hidden.append(hidden)
        act_list.append(group_gram(normed))
        if layer_index + 1 < LAYERS:
            product = jnp.dot(normed.reshape(-1, D), weights[slot_pick, section_pick], preferred_element_type=jnp.float32)
            product = product.astype(jnp.bfloat16).reshape(hidden.shape)
            hidden = (hidden_wide + product.astype(jnp.float32)).astype(jnp.bfloat16)
    delta = cotangent
    grad_list = [None] * LAYERS
    for layer_index in reversed(range(LAYERS)):
        grad_list[layer_index] = group_gram(delta)
        if layer_index > 0:
            slot_pick = layer_index // N_PIPE
            section_pick = layer_index % N_PIPE
            weight = weights[slot_pick, section_pick]
            gain_row = norm_gains[slot_pick, section_pick]
            flat_delta = delta.reshape(-1, D)
            back_sum = jnp.zeros(flat_delta.shape, jnp.float32)
            for column in range(N_TENSOR):
                lower = column * quarter
                upper = lower + quarter
                term = lax.dot_general(flat_delta[:, lower:upper], weight[:, lower:upper], (((1,), (1,)), ((), ())), preferred_element_type=jnp.float32)
                back_sum = back_sum + rounded(term)
            back_sum = back_sum.reshape(delta.shape)
            hidden_wide, inverse_rms, normed = normalize(saved_hidden[layer_index], gain_row)
            scaled = gain_row * back_sum
            inner = lax.optimization_barrier(jnp.mean(hidden_wide * scaled, axis=-1, keepdims=True))
            delta = (delta.astype(jnp.float32) + inverse_rms * scaled - inverse_rms ** 3 * hidden_wide * inner).astype(jnp.bfloat16)
    act_factor = jnp.stack(act_list, 0).reshape(SLOTS, N_PIPE, D, D).transpose(2, 0, 1, 3)
    grad_factor = jnp.stack(grad_list, 0).reshape(SLOTS, N_PIPE, D, D).transpose(2, 0, 1, 3)
    return (act_factor, grad_factor)
```

```python
import functools

import jax
import jax.numpy as jnp
from jax import lax
from jax.experimental import pallas as pl
from jax.experimental.pallas import tpu as pltpu
from jax.sharding import Mesh
from jax.sharding import PartitionSpec as P

DP = ("dp_0", "dp_1")
TENSOR_DP = ("tensor", "dp_0", "dp_1")
AXES = ("pipe", "tensor", "dp_0", "dp_1")
SIZES = (4, 4, 2, 4)
EPSILON = 1e-05
PIPES = 4
LAYERS = 8
STREAMS = 2
LAST = LAYERS - 1
F32 = jnp.float32
BF16 = jnp.bfloat16
ANYWHERE = pl.BlockSpec(memory_space=pl.ANY)


def flat(place):
    index = 0
    for size, at in zip(SIZES, place):
        index = index * size + at
    return index


def permuted(array, target):
    pairs = []
    for pipe in range(SIZES[0]):
        for tensor in range(SIZES[1]):
            for z in range(SIZES[2]):
                for y in range(SIZES[3]):
                    there = target(pipe, tensor, z, y)
                    if there is not None:
                        pairs.append((flat((pipe, tensor, z, y)), flat(there)))
    return lax.ppermute(array, AXES, pairs)


def forward_moves(tick):
    moves = {}
    for stream in range(STREAMS):
        layer = tick - stream
        if 0 <= layer < LAST:
            source = layer % PIPES
            moves[source] = ((layer + 1) % PIPES, source % 2)
    return moves


def backward_moves(tick):
    moves = {}
    for stream in range(STREAMS):
        layer = 2 * LAST + stream - tick
        if 1 <= layer <= LAST:
            source = layer % PIPES
            moves[source] = ((layer - 1) % PIPES, 1 - source % 2)
    return moves


def fan_out(arrays, moves):
    received = []
    for step, array in enumerate(arrays):

        def target(pipe, tensor, z, y, step=step):
            if pipe not in moves:
                return None
            there, flip = moves[pipe]
            return (there, (tensor + step) % SIZES[1], z ^ flip, y)

        received.append(permuted(array, target))
    return received


def forward_place(tick, pipe):
    stream = lax.rem(tick - pipe + PIPES, PIPES)
    layer = tick - stream
    active = (stream < STREAMS) & (layer >= 0) & (layer < LAYERS)
    slot = jnp.where(active & (layer >= PIPES), 1, 0)
    return active, slot, jnp.where(active, stream, 0), active & (layer < LAST)


def backward_place(tick, pipe):
    stream = lax.rem(pipe + tick + 2 * PIPES - 2 * LAST % PIPES, PIPES)
    layer = 2 * LAST + stream - tick
    active = (stream < STREAMS) & (layer >= 0) & (layer < LAYERS)
    slot = jnp.where(active & (layer >= PIPES), 1, 0)
    return active, slot, jnp.where(active, stream, 0), active & (layer > 0)


def turned(index, count=4):
    return lax.rem(index + count, count)


def ingest(meta, arrays):
    rows, features = arrays[0].shape
    half = rows // 2
    quarter = features // 4

    def kernel(meta_ref, *refs):
        sources, (hidden_ref, cotangent_ref) = refs[:4], refs[4:]
        tensor = meta_ref[1]
        for step in range(4):
            row = pl.multiple_of(turned(tensor - step) * half, half)
            for stream in range(2):
                for turn in range(4):
                    column = pl.multiple_of(turned(tensor - turn) * quarter, quarter)
                    piece = sources[step][stream * half : (stream + 1) * half, pl.ds(column, quarter)]
                    hidden_ref[stream, turn, pl.ds(row, half), :] = piece
                    if turn == 0:
                        cotangent_ref[stream, pl.ds(row, half), :] = piece.astype(F32)

    whole = pl.BlockSpec(memory_space=pltpu.VMEM)
    return pl.pallas_call(
        kernel,
        in_specs=[pl.BlockSpec(memory_space=pltpu.SMEM)] + [whole] * 4,
        out_specs=[whole, whole],
        out_shape=[
            jax.ShapeDtypeStruct((2, 4, 4 * half, quarter), BF16),
            jax.ShapeDtypeStruct((2, 4 * half, quarter), F32),
        ],
        name="ingest",
    )(meta, *arrays)


def forward_step(tick, meta, blocks, gains, weights, hidden_stash, normed_stash):
    rows, quarter = blocks[0].shape
    features = 4 * quarter

    def kernel(meta_ref, b0, b1, b2, b3, gain_ref, weight_ref, *refs):
        next_ref, hidden_ref, normed_ref, normed, total = refs[-5:]
        turn = pl.program_id(0)
        tensor = meta_ref[1]
        active, slot, _, multiplies = forward_place(tick, meta_ref[0])
        ins = (b0, b1, b2, b3)

        @pl.when(active & (turn == 0))
        def _():
            squares = 0.0
            for ref in ins:
                wide = ref[...].astype(F32)
                squares = squares + jnp.sum(wide * wide, axis=-1, keepdims=True)
            scale = lax.rsqrt(squares * (1.0 / features) + EPSILON)
            for k, ref in enumerate(ins):
                gain = gain_ref[slot, pl.ds(turned(tensor - k), 1), :]
                normed[k] = (ref[...].astype(F32) * scale * gain).astype(BF16)
                hidden_ref[0, k] = ref[...]
            normed_ref[0] = normed[0]

        @pl.when(multiplies)
        def _():
            part = jnp.dot(normed[turn], weight_ref[0], preferred_element_type=F32)

            @pl.when(turn == 0)
            def _():
                total[...] = part

            @pl.when(turn > 0)
            def _():
                total[...] += part

        @pl.when(multiplies & (turn == 3))
        def _():
            rounded = total[...].astype(BF16).astype(F32)
            next_ref[...] = (b0[...].astype(F32) + rounded).astype(BF16)

    def weight_at(turn, meta_ref):
        _, slot, _, multiplies = forward_place(tick, meta_ref[0])
        return slot, jnp.where(multiplies, turned(meta_ref[1] - turn), 0), 0

    def stash_at(turn, meta_ref):
        active, slot, stream, _ = forward_place(tick, meta_ref[0])
        return jnp.where(active, slot * 2 + stream, 4)

    block = pl.BlockSpec((rows, quarter), lambda turn, meta_ref: (0, 0))
    stashes = [] if hidden_stash is None else [hidden_stash, normed_stash]
    return pl.pallas_call(
        kernel,
        grid_spec=pltpu.PrefetchScalarGridSpec(
            num_scalar_prefetch=1,
            grid=(4,),
            in_specs=[block] * 4
            + [
                pl.BlockSpec((2, 4, quarter), lambda turn, meta_ref: (0, 0, 0)),
                pl.BlockSpec((1, quarter, quarter), weight_at),
            ]
            + [ANYWHERE] * len(stashes),
            out_specs=[
                block,
                pl.BlockSpec((1, 4, rows, quarter), lambda turn, m: (stash_at(turn, m), 0, 0, 0)),
                pl.BlockSpec((1, rows, quarter), lambda turn, m: (stash_at(turn, m), 0, 0)),
            ],
            scratch_shapes=[pltpu.VMEM((4, rows, quarter), BF16), pltpu.VMEM((rows, quarter), F32)],
        ),
        out_shape=[
            jax.ShapeDtypeStruct((rows, quarter), BF16),
            jax.ShapeDtypeStruct((5, 4, rows, quarter), BF16),
            jax.ShapeDtypeStruct((5, rows, quarter), BF16),
        ],
        input_output_aliases={7: 1, 8: 2} if stashes else {},
        compiler_params=pltpu.CompilerParams(vmem_limit_bytes=24 << 20),
        cost_estimate=pl.CostEstimate(
            flops=2 * rows * features * quarter, bytes_accessed=2 * features * quarter, transcendentals=0
        ),
        name="forward_step",
    )(meta, *blocks, gains, weights, *stashes)


def backward_step(tick, meta, own, others, gains, weights, hidden_stash, grad_stash):
    rows, quarter = own.shape
    features = 4 * quarter

    def kernel(meta_ref, own_ref, c1, c2, c3, gain_ref, weight_ref, hidden_ref, *refs):
        own_out, o1, o2, o3, grad_ref, delta, scaled, inner = refs[-8:]
        turn = pl.program_id(0)
        tensor = meta_ref[1]
        active, slot, _, multiplies = backward_place(tick, meta_ref[0])

        @pl.when(active & (turn == 0))
        def _():
            total = own_ref[...]
            for ref in (c1, c2, c3):
                total = total + ref[...].astype(F32)
            delta[...] = total.astype(BF16)
            grad_ref[0] = total.astype(BF16)

        @pl.when(multiplies)
        def _():
            part = lax.dot_general(
                delta[...], weight_ref[0], (((1,), (1,)), ((), ())), preferred_element_type=F32
            )
            gain = gain_ref[slot, pl.ds(turned(tensor + turn), 1), :]
            back = part.astype(BF16).astype(F32) * gain
            scaled[turn] = back
            hidden = hidden_ref[0, turned(-turn)].astype(F32)
            sums = jnp.broadcast_to(jnp.sum(hidden * back, axis=-1, keepdims=True), inner.shape)

            @pl.when(turn == 0)
            def _():
                inner[...] = sums

            @pl.when(turn > 0)
            def _():
                inner[...] += sums

        @pl.when(multiplies & (turn == 3))
        def _():
            squares = 0.0
            for k in range(4):
                wide = hidden_ref[0, k].astype(F32)
                squares = squares + jnp.sum(wide * wide, axis=-1, keepdims=True)
            scale = lax.rsqrt(squares * (1.0 / features) + EPSILON)
            slope = scale * scale * scale * (inner[:, :1] * (1.0 / features))
            for k, ref in enumerate((own_out, o1, o2, o3)):
                change = scale * scaled[k] - slope * hidden_ref[0, (4 - k) % 4].astype(F32)
                if k == 0:
                    ref[...] = delta[...].astype(F32) + change
                else:
                    ref[...] = change.astype(BF16)

    def weight_at(turn, meta_ref):
        _, slot, _, multiplies = backward_place(tick, meta_ref[0])
        return slot, jnp.where(multiplies, turned(meta_ref[1] + turn), 0), 0

    def stash_at(turn, meta_ref, idle):
        active, slot, stream, _ = backward_place(tick, meta_ref[0])
        return jnp.where(active, slot * 2 + stream, idle)

    block = pl.BlockSpec((rows, quarter), lambda turn, meta_ref: (0, 0))
    stashes = [] if grad_stash is None else [grad_stash]
    return pl.pallas_call(
        kernel,
        grid_spec=pltpu.PrefetchScalarGridSpec(
            num_scalar_prefetch=1,
            grid=(4,),
            in_specs=[block] * 4
            + [
                pl.BlockSpec((2, 4, quarter), lambda turn, meta_ref: (0, 0, 0)),
                pl.BlockSpec((1, quarter, quarter), weight_at),
                pl.BlockSpec((1, 4, rows, quarter), lambda turn, m: (stash_at(turn, m, 0), 0, 0, 0)),
            ]
            + [ANYWHERE] * len(stashes),
            out_specs=[block] * 4
            + [pl.BlockSpec((1, rows, quarter), lambda turn, m: (stash_at(turn, m, 4), 0, 0))],
            scratch_shapes=[
                pltpu.VMEM((rows, quarter), BF16),
                pltpu.VMEM((4, rows, quarter), F32),
                pltpu.VMEM((rows, 128), F32),
            ],
        ),
        out_shape=[jax.ShapeDtypeStruct((rows, quarter), F32)]
        + [jax.ShapeDtypeStruct((rows, quarter), BF16)] * 3
        + [jax.ShapeDtypeStruct((5, rows, quarter), BF16)],
        input_output_aliases={8: 4} if stashes else {},
        compiler_params=pltpu.CompilerParams(vmem_limit_bytes=24 << 20),
        cost_estimate=pl.CostEstimate(
            flops=2 * rows * features * quarter, bytes_accessed=2 * features * quarter, transcendentals=0
        ),
        name="backward_step",
    )(meta, own, *others, gains, weights, hidden_stash, *stashes)


def gram(meta, tokens, picked, inv_tokens):
    slots, count, quarter = tokens.shape
    own = picked.shape[-1]

    def kernel(meta_ref, tokens_ref, picked_ref, *outs):
        for step, out in enumerate(outs):
            left = picked_ref[0, turned(meta_ref[1] + step)]
            product = lax.dot_general(
                left, tokens_ref[0], (((0,), (0,)), ((), ())), preferred_element_type=F32
            )
            out[0] = (product * inv_tokens).astype(BF16)

    return pl.pallas_call(
        kernel,
        grid_spec=pltpu.PrefetchScalarGridSpec(
            num_scalar_prefetch=1,
            grid=(slots,),
            in_specs=[
                pl.BlockSpec((1, count, quarter), lambda s, m: (s, 0, 0)),
                pl.BlockSpec((1, 4, count, own), lambda s, m: (s, 0, 0, 0)),
            ],
            out_specs=[pl.BlockSpec((1, own, quarter), lambda s, m: (s, 0, 0))] * 4,
        ),
        out_shape=[jax.ShapeDtypeStruct((slots, own, quarter), BF16)] * 4,
        compiler_params=pltpu.CompilerParams(vmem_limit_bytes=32 << 20),
        cost_estimate=pl.CostEstimate(
            flops=2 * slots * count * 4 * own * quarter,
            bytes_accessed=2 * slots * (count * quarter + 8 * own * quarter),
            transcendentals=0,
        ),
        name="gram",
    )(meta, tokens, picked)


def share_columns(blocks):
    return [blocks[0]] + [
        permuted(block, lambda p, t, z, y, k=k: (p, (t + k) % SIZES[1], z, y))
        for k, block in enumerate(blocks)
        if k
    ]


def assemble(meta, first, second):
    own, quarter = first[0].shape

    def kernel(meta_ref, *refs):
        out = refs[8]
        tensor = meta_ref[1]
        for step in range(4):
            column = pl.multiple_of(turned(tensor - step) * quarter, quarter)
            out[:, :, pl.ds(column, quarter)] = jnp.stack([refs[step][...], refs[4 + step][...]], 1)

    whole = pl.BlockSpec(memory_space=pltpu.VMEM)
    return pl.pallas_call(
        kernel,
        in_specs=[pl.BlockSpec(memory_space=pltpu.SMEM)] + [whole] * 8,
        out_specs=whole,
        out_shape=jax.ShapeDtypeStruct((own, 2, 4 * quarter), BF16),
        compiler_params=pltpu.CompilerParams(vmem_limit_bytes=32 << 20),
        name="assemble",
    )(meta, *first, *second)


def body(inputs, weights, norm_gains, cotangent):
    micro_count, shard_rows, features = inputs.shape
    quarter = weights.shape[3]
    pipe = lax.axis_index("pipe")
    tensor = lax.axis_index("tensor")
    group = lax.axis_index(DP)
    own_rows = quarter // lax.axis_size(DP)
    inv_tokens = 1.0 / (micro_count * shard_rows * lax.axis_size(TENSOR_DP))
    meta = jnp.stack([pipe, tensor]).astype(jnp.int32)
    weights = weights.reshape(weights.shape[0], features, quarter)
    gains = norm_gains.reshape(norm_gains.shape[0], 4, quarter)

    def start_target(step):
        def target(p, t, z, y):
            if p == 0 and step:
                return (p, (t + step) % SIZES[1], z, y)
            if p == LAST % PIPES:
                return (p, (t + step) % SIZES[1], 1 - z, y)
            return None

        return target

    given = jnp.where(pipe == LAST % PIPES, cotangent, inputs).reshape(-1, features)
    arrived = [permuted(given, start_target(step)) for step in range(4)]
    arrived[0] = jnp.where(pipe == 0, given, arrived[0])
    first_blocks, last_deltas = ingest(meta, arrived)

    def gather_group(rows):
        return lax.all_gather(rows, DP, axis=0, tiled=True)

    def pick(tokens):
        mine = lax.dynamic_slice_in_dim(tokens, group * own_rows, own_rows, 1)
        return lax.all_gather(mine, "tensor", axis=0, tiled=False)

    def factor_blocks(tokens_list):
        tokens = jnp.stack(tokens_list)
        picked = jnp.stack([pick(one) for one in tokens_list])
        return share_columns(gram(meta, tokens, picked, inv_tokens))

    hidden_stash = normed_stash = grad_stash = None
    zeros = jnp.zeros(first_blocks.shape[2:], BF16)
    received = [first_blocks[0, k] for k in range(4)]
    back = [jnp.zeros(first_blocks.shape[2:], F32), zeros, zeros, zeros]
    act_tokens = []
    for tick in range(2 * LAST + STREAMS):
        if tick <= LAST + 1:
            blocks = received
            if 0 < tick < STREAMS:
                blocks = [jnp.where(pipe == 0, first_blocks[tick, k], received[k]) for k in range(4)]
            following, hidden_stash, normed_stash = forward_step(
                tick, meta, blocks, gains, weights, hidden_stash, normed_stash
            )
            if tick <= LAST:
                received = fan_out([following] * 4, forward_moves(tick))
            if tick == PIPES:
                act_tokens.append(gather_group(normed_stash[:2].reshape(-1, quarter)))
            if tick == 2 * PIPES:
                act_tokens.append(gather_group(normed_stash[2:4].reshape(-1, quarter)))
        if tick >= LAST:
            own = back[0]
            if tick < LAST + STREAMS:
                own = jnp.where(pipe == LAST % PIPES, last_deltas[tick - LAST], own)
            *sent, grad_stash = backward_step(
                tick, meta, own, back[1:], gains, weights, hidden_stash, grad_stash
            )
            if tick < 2 * LAST + STREAMS - 1:
                back = fan_out(sent, backward_moves(tick))
            if tick == LAST + PIPES:
                late_tokens = gather_group(grad_stash[2:4].reshape(-1, quarter))
    act_blocks = factor_blocks(act_tokens)
    act_factor = assemble(meta, [b[0] for b in act_blocks], [b[1] for b in act_blocks])
    late = factor_blocks([late_tokens])
    early = factor_blocks([gather_group(grad_stash[:2].reshape(-1, quarter))])
    grad_factor = assemble(meta, [b[0] for b in early], [b[0] for b in late])
    shape = (own_rows, 2, 1, features)
    return (act_factor.reshape(shape), grad_factor.reshape(shape))


def solution(mesh):
    split = Mesh(mesh.devices.reshape(SIZES), AXES)
    placed = (
        P(None, TENSOR_DP, None),
        P(None, "pipe", None, "tensor"),
        P(None, "pipe", None),
        P(None, TENSOR_DP, None),
    )
    return jax.shard_map(
        body,
        mesh=split,
        in_specs=placed,
        out_specs=(P(TENSOR_DP, None, "pipe", None), P(TENSOR_DP, None, "pipe", None)),
        check_vma=False,
    )
```

```python
import functools

import jax
import jax.numpy as jnp
from jax import lax
from jax.experimental import pallas as pl
from jax.experimental.pallas import tpu as pltpu
from jax.sharding import Mesh
from jax.sharding import PartitionSpec as P

DP = ("dp_0", "dp_1")
TENSOR_DP = ("tensor", "dp_0", "dp_1")
AXES = ("pipe", "tensor", "dp_0", "dp_1")
SIZES = (4, 4, 2, 4)
EPSILON = 1e-05
PIPES = 4
LAYERS = 8
STREAMS = 2
LAST = LAYERS - 1
F32 = jnp.float32
BF16 = jnp.bfloat16
ANYWHERE = pl.BlockSpec(memory_space=pl.ANY)


def flat(place):
    index = 0
    for size, at in zip(SIZES, place):
        index = index * size + at
    return index


def permuted(array, target):
    pairs = []
    for pipe in range(SIZES[0]):
        for tensor in range(SIZES[1]):
            for z in range(SIZES[2]):
                for y in range(SIZES[3]):
                    there = target(pipe, tensor, z, y)
                    if there is not None:
                        pairs.append((flat((pipe, tensor, z, y)), flat(there)))
    return lax.ppermute(array, AXES, pairs)


def forward_moves(tick):
    moves = {0: (1, 0), 2: (3, 0)}
    moves.update({3: (0, 1)} if tick % PIPES in (0, 3) else {1: (2, 1)})
    return moves


def backward_moves(tick):
    moves = {1: (0, 0), 3: (2, 0)}
    moves.update({0: (3, 1)} if (2 * LAST - tick) % PIPES in (0, 3) else {2: (1, 1)})
    return moves


def fan_out(arrays, moves):
    received = []
    for step, array in enumerate(arrays):

        def target(pipe, tensor, z, y, step=step):
            if pipe not in moves:
                return None
            there, flip = moves[pipe]
            return (there, (tensor + step) % SIZES[1], z ^ flip, y)

        received.append(permuted(array, target))
    return received


def forward_place(tick, pipe):
    stream = lax.rem(tick - pipe + PIPES, PIPES)
    layer = tick - stream
    active = (stream < STREAMS) & (layer >= 0) & (layer < LAYERS)
    slot = jnp.where(active & (layer >= PIPES), 1, 0)
    return active, slot, jnp.where(active, stream, 0), active & (layer < LAST)


def backward_place(tick, pipe):
    stream = lax.rem(pipe + tick + 2 * PIPES - 2 * LAST % PIPES, PIPES)
    layer = 2 * LAST + stream - tick
    active = (stream < STREAMS) & (layer >= 0) & (layer < LAYERS)
    slot = jnp.where(active & (layer >= PIPES), 1, 0)
    return active, slot, jnp.where(active, stream, 0), active & (layer > 0)


def turned(index, count=4):
    return lax.rem(index + count, count)


def held(weights, after):
    pieces = 8
    rows = weights.shape[1] // pieces

    def kernel(source, *refs):
        target, sems = refs[-2:]
        copies = []
        for slot in range(weights.shape[0]):
            for k in range(pieces):
                part = pl.ds(k * rows, rows)
                copies.append(
                    pltpu.make_async_copy(
                        source.at[slot, part], target.at[slot, part], sems.at[slot, k]
                    )
                )
        for copy in copies:
            copy.start()
        for copy in copies:
            copy.wait()

    return pl.pallas_call(
        kernel,
        in_specs=[ANYWHERE] * (1 + len(after)),
        out_specs=pl.BlockSpec(memory_space=pltpu.VMEM),
        out_shape=pltpu.VMEM(weights.shape, weights.dtype),
        scratch_shapes=[pltpu.SemaphoreType.DMA((weights.shape[0], pieces))],
        compiler_params=pltpu.CompilerParams(vmem_limit_bytes=17 << 20),
        name="held",
    )(pltpu.with_memory_space_constraint(weights, pltpu.HBM), *after)


def ingest(meta, arrays):
    rows, features = arrays[0].shape
    half = rows // 2
    quarter = features // 4

    def kernel(meta_ref, *refs):
        sources, blocks, own_ref = refs[:4], refs[4:12], refs[12]
        tensor = meta_ref[1]
        for step in range(4):
            row = pl.multiple_of(turned(tensor - step) * half, half)
            for stream in range(2):
                for turn in range(4):
                    column = pl.multiple_of(turned(tensor - turn) * quarter, quarter)
                    piece = sources[step][stream * half : (stream + 1) * half, pl.ds(column, quarter)]
                    blocks[4 * stream + turn][pl.ds(row, half), :] = piece
                    if turn == 0:
                        own_ref[stream, pl.ds(row, half), :] = piece

    whole = pl.BlockSpec(memory_space=pltpu.VMEM)
    return pl.pallas_call(
        kernel,
        in_specs=[pl.BlockSpec(memory_space=pltpu.SMEM)] + [whole] * 4,
        out_specs=[whole] * 9,
        out_shape=[jax.ShapeDtypeStruct((4 * half, quarter), BF16)] * 8
        + [jax.ShapeDtypeStruct((2, 4 * half, quarter), BF16)],
        compiler_params=pltpu.CompilerParams(vmem_limit_bytes=8 << 20),
        name="ingest",
    )(meta, *arrays)


def forward_step(tick, meta, blocks, firsts, gains, weights, hidden_stash, normed_stash, after=()):
    rows, quarter = blocks[0].shape
    features = 4 * quarter

    def kernel(meta_ref, b0, b1, b2, b3, gain_ref, weight_ref, *refs):
        next_ref, hidden_ref, normed_ref, normed, total = refs[-5:]
        turn = pl.program_id(0)
        tensor = meta_ref[1]
        active, slot, _, multiplies = forward_place(tick, meta_ref[0])

        @pl.when(active & (turn == 0))
        def _():
            for k, ref in enumerate((b0, b1, b2, b3)):
                block = ref[...]
                if firsts:
                    block = jnp.where(meta_ref[0] == 0, refs[k][...], block)
                hidden_ref[0, k] = block
            squares = 0.0
            for k in range(4):
                wide = hidden_ref[0, k].astype(F32)
                squares = squares + jnp.sum(wide * wide, axis=-1, keepdims=True)
            scale = lax.rsqrt(squares * (1.0 / features) + EPSILON)
            for k in range(4):
                gain = gain_ref[slot, pl.ds(turned(tensor - k), 1), :]
                normed[k] = (hidden_ref[0, k].astype(F32) * scale * gain).astype(BF16)
            normed_ref[0] = normed[0]

        @pl.when(multiplies)
        def _():
            part = jnp.dot(normed[turn], weight_ref[0], preferred_element_type=F32)

            @pl.when(turn == 0)
            def _():
                total[...] = part

            @pl.when(turn > 0)
            def _():
                total[...] += part

        @pl.when(multiplies & (turn == 3))
        def _():
            rounded = total[...].astype(BF16).astype(F32)
            next_ref[...] = (hidden_ref[0, 0].astype(F32) + rounded).astype(BF16)

    def weight_at(turn, meta_ref):
        _, slot, _, multiplies = forward_place(tick, meta_ref[0])
        return slot, jnp.where(multiplies, turned(meta_ref[1] - turn), 0), 0

    def stash_at(turn, meta_ref):
        active, slot, stream, _ = forward_place(tick, meta_ref[0])
        return jnp.where(active, slot * 2 + stream, 4)

    block = pl.BlockSpec((rows, quarter), lambda turn, meta_ref: (0, 0))
    stashes = [] if hidden_stash is None else [hidden_stash, normed_stash]
    return pl.pallas_call(
        kernel,
        grid_spec=pltpu.PrefetchScalarGridSpec(
            num_scalar_prefetch=1,
            grid=(4,),
            in_specs=[block] * 4
            + [
                pl.BlockSpec((2, 4, quarter), lambda turn, meta_ref: (0, 0, 0)),
                pl.BlockSpec((1, quarter, quarter), weight_at),
            ]
            + [block] * len(firsts)
            + [ANYWHERE] * (len(stashes) + len(after)),
            out_specs=[
                block,
                pl.BlockSpec((1, 4, rows, quarter), lambda turn, m: (stash_at(turn, m), 0, 0, 0)),
                pl.BlockSpec((1, rows, quarter), lambda turn, m: (stash_at(turn, m), 0, 0)),
            ],
            scratch_shapes=[pltpu.VMEM((4, rows, quarter), BF16), pltpu.VMEM((rows, quarter), F32)],
        ),
        out_shape=[
            jax.ShapeDtypeStruct((rows, quarter), BF16),
            jax.ShapeDtypeStruct((5, 4, rows, quarter), BF16),
            jax.ShapeDtypeStruct((5, rows, quarter), BF16),
        ],
        input_output_aliases={7 + len(firsts): 1, 8 + len(firsts): 2} if stashes else {},
        compiler_params=pltpu.CompilerParams(vmem_limit_bytes=16 << 20),
        cost_estimate=pl.CostEstimate(
            flops=2 * rows * features * quarter, bytes_accessed=2 * features * quarter, transcendentals=0
        ),
        name="forward_step",
    )(meta, *blocks, gains, weights, *firsts, *stashes, *after)


def backward_step(tick, meta, given, own, others, gains, weights, hidden_stash, grad_stash, after=()):
    rows, quarter = own.shape
    features = 4 * quarter

    def kernel(meta_ref, given_ref, own_ref, c1, c2, c3, gain_ref, weight_ref, hidden_ref, *refs):
        own_out, o1, o2, o3, grad_ref, delta, scaled, inner = refs[-8:]
        turn = pl.program_id(0)
        tensor = meta_ref[1]
        active, slot, stream, multiplies = backward_place(tick, meta_ref[0])
        starts = active & (tick < LAST + STREAMS) & (meta_ref[0] == LAST % PIPES)

        @pl.when(starts & (turn == 0))
        def _():
            delta[...] = given_ref[stream]
            grad_ref[0] = given_ref[stream]

        @pl.when(active & jnp.logical_not(starts) & (turn == 0))
        def _():
            total = own_ref[...]
            for ref in (c1, c2, c3):
                total = total + ref[...].astype(F32)
            delta[...] = total.astype(BF16)
            grad_ref[0] = total.astype(BF16)

        @pl.when(multiplies)
        def _():
            part = lax.dot_general(
                delta[...], weight_ref[0], (((1,), (1,)), ((), ())), preferred_element_type=F32
            )
            gain = gain_ref[slot, pl.ds(turned(tensor + turn), 1), :]
            back = part.astype(BF16).astype(F32) * gain
            scaled[turn] = back
            hidden = hidden_ref[0, turned(-turn)].astype(F32)
            sums = jnp.broadcast_to(jnp.sum(hidden * back, axis=-1, keepdims=True), inner.shape)

            @pl.when(turn == 0)
            def _():
                inner[...] = sums

            @pl.when(turn > 0)
            def _():
                inner[...] += sums

        @pl.when(multiplies & (turn == 3))
        def _():
            squares = 0.0
            for k in range(4):
                wide = hidden_ref[0, k].astype(F32)
                squares = squares + jnp.sum(wide * wide, axis=-1, keepdims=True)
            scale = lax.rsqrt(squares * (1.0 / features) + EPSILON)
            slope = scale * scale * scale * (inner[:, :1] * (1.0 / features))
            for k, ref in enumerate((own_out, o1, o2, o3)):
                change = scale * scaled[k] - slope * hidden_ref[0, (4 - k) % 4].astype(F32)
                if k == 0:
                    ref[...] = delta[...].astype(F32) + change
                else:
                    ref[...] = change.astype(BF16)

    def weight_at(turn, meta_ref):
        _, slot, _, multiplies = backward_place(tick, meta_ref[0])
        return slot, jnp.where(multiplies, turned(meta_ref[1] + turn), 0), 0

    def stash_at(turn, meta_ref, idle):
        active, slot, stream, _ = backward_place(tick, meta_ref[0])
        return jnp.where(active, slot * 2 + stream, idle)

    block = pl.BlockSpec((rows, quarter), lambda turn, meta_ref: (0, 0))
    stashes = [] if grad_stash is None else [grad_stash]
    return pl.pallas_call(
        kernel,
        grid_spec=pltpu.PrefetchScalarGridSpec(
            num_scalar_prefetch=1,
            grid=(4,),
            in_specs=[pl.BlockSpec((2, rows, quarter), lambda turn, meta_ref: (0, 0, 0))]
            + [block] * 4
            + [
                pl.BlockSpec((2, 4, quarter), lambda turn, meta_ref: (0, 0, 0)),
                pl.BlockSpec((1, quarter, quarter), weight_at),
                pl.BlockSpec((1, 4, rows, quarter), lambda turn, m: (stash_at(turn, m, 0), 0, 0, 0)),
            ]
            + [ANYWHERE] * (len(stashes) + len(after)),
            out_specs=[block] * 4
            + [pl.BlockSpec((1, rows, quarter), lambda turn, m: (stash_at(turn, m, 4), 0, 0))],
            scratch_shapes=[
                pltpu.VMEM((rows, quarter), BF16),
                pltpu.VMEM((4, rows, quarter), F32),
                pltpu.VMEM((rows, 128), F32),
            ],
        ),
        out_shape=[jax.ShapeDtypeStruct((rows, quarter), F32)]
        + [jax.ShapeDtypeStruct((rows, quarter), BF16)] * 3
        + [jax.ShapeDtypeStruct((5, rows, quarter), BF16)],
        input_output_aliases={9: 4} if stashes else {},
        compiler_params=pltpu.CompilerParams(vmem_limit_bytes=16 << 20),
        cost_estimate=pl.CostEstimate(
            flops=2 * rows * features * quarter, bytes_accessed=2 * features * quarter, transcendentals=0
        ),
        name="backward_step",
    )(meta, given, own, *others, gains, weights, hidden_stash, *stashes, *after)


def own_columns(meta, pieces, own):
    rows = pieces[0].shape[0]

    def kernel(meta_ref, *refs):
        column = pl.multiple_of(meta_ref[2] * own, own)
        for k, piece in enumerate(refs[:-1]):
            refs[-1][k * rows : (k + 1) * rows, :] = piece[:, pl.ds(column, own)]

    whole = pl.BlockSpec(memory_space=pltpu.VMEM)
    return pl.pallas_call(
        kernel,
        in_specs=[pl.BlockSpec(memory_space=pltpu.SMEM)] + [whole] * len(pieces),
        out_specs=whole,
        out_shape=jax.ShapeDtypeStruct((rows * len(pieces), own), BF16),
        compiler_params=pltpu.CompilerParams(vmem_limit_bytes=8 << 20),
        name="own_columns",
    )(meta, *pieces)


def gram(pieces, picked, inv_tokens):
    quarter = pieces[0].shape[-1]
    count, own = picked[0].shape
    starts = [0]
    for piece in pieces:
        starts.append(starts[-1] + piece.shape[0])

    def kernel(*refs):
        token_refs, picked_refs, outs = refs[: len(pieces)], refs[len(pieces) : -4], refs[-4:]
        for left, out in zip(picked_refs, outs):
            product = 0.0
            for ref, start, stop in zip(token_refs, starts, starts[1:]):
                product = product + lax.dot_general(
                    left[start:stop, :], ref[...], (((0,), (0,)), ((), ())), preferred_element_type=F32
                )
            out[...] = (product * inv_tokens).astype(BF16)

    whole = pl.BlockSpec(memory_space=pltpu.VMEM)
    return pl.pallas_call(
        kernel,
        in_specs=[whole] * (len(pieces) + 4),
        out_specs=[whole] * 4,
        out_shape=[jax.ShapeDtypeStruct((own, quarter), BF16)] * 4,
        compiler_params=pltpu.CompilerParams(vmem_limit_bytes=20 << 20),
        cost_estimate=pl.CostEstimate(
            flops=2 * count * 4 * own * quarter,
            bytes_accessed=2 * (count * quarter + 8 * own * quarter),
            transcendentals=0,
        ),
        name="gram",
    )(*pieces, *picked)


def shifted(array, x=0, y=0, z=0):
    return permuted(array, lambda p, t, u, v: (p, (t + x) % SIZES[1], u ^ z, (v + y) % SIZES[3]))


def share_columns(blocks):
    return [blocks[0]] + [shifted(blocks[4 - k], x=k) for k in (1, 2, 3)]


def assemble(meta, first, second):
    own, quarter = first[0].shape

    def kernel(meta_ref, *refs):
        out = refs[8]
        tensor = meta_ref[1]
        for step in range(4):
            column = pl.multiple_of(turned(tensor - step) * quarter, quarter)
            out[:, :, pl.ds(column, quarter)] = jnp.stack([refs[step][...], refs[4 + step][...]], 1)

    whole = pl.BlockSpec(memory_space=pltpu.VMEM)
    return pl.pallas_call(
        kernel,
        in_specs=[pl.BlockSpec(memory_space=pltpu.SMEM)] + [whole] * 8,
        out_specs=whole,
        out_shape=jax.ShapeDtypeStruct((own, 2, 4 * quarter), BF16),
        compiler_params=pltpu.CompilerParams(vmem_limit_bytes=20 << 20),
        name="assemble",
    )(meta, *first, *second)


def body(inputs, weights, norm_gains, cotangent):
    micro_count, shard_rows, features = inputs.shape
    quarter = weights.shape[3]
    pipe = lax.axis_index("pipe")
    tensor = lax.axis_index("tensor")
    group = lax.axis_index(DP)
    own_rows = quarter // lax.axis_size(DP)
    inv_tokens = 1.0 / (micro_count * shard_rows * lax.axis_size(TENSOR_DP))
    meta = jnp.stack([pipe, tensor, group]).astype(jnp.int32)
    gains = norm_gains.reshape(norm_gains.shape[0], 4, quarter)
    weights = held(weights.reshape(weights.shape[0], features, quarter), (meta, gains))
    weights = pltpu.with_memory_space_constraint(weights, pltpu.VMEM)

    given = jnp.where(pipe == LAST % PIPES, cotangent, inputs).reshape(-1, features)
    *first_blocks, last_deltas = ingest(meta, [given] + [shifted(given, x=k) for k in (1, 2, 3)])
    last_deltas = shifted(last_deltas, z=1)

    def picked_rows(pieces):
        mine = own_columns(meta, pieces, own_rows)
        return [mine] + [shifted(mine, x=k) for k in (1, 2, 3)]

    def over_z(rows):
        return jnp.concatenate([rows, shifted(rows, z=1)])

    def over_y(rows):
        return [rows] + [shifted(rows, y=k) for k in (1, 2, 3)]

    def slot_rows(stash, slot):
        return stash[2 * slot : 2 * slot + 2].reshape(-1, quarter)

    def blocks_of(pieces, picked):
        return share_columns(gram(pieces, picked, inv_tokens))

    hidden_stash = normed_stash = grad_stash = None
    received = first_blocks[:4]
    back = [jnp.zeros(first_blocks[0].shape, F32)] + first_blocks[1:4]
    after = {}
    for tick in range(2 * LAST + STREAMS):
        waits = after.get(tick, ())
        if tick <= LAST + 1:
            firsts = first_blocks[4 * tick : 4 * tick + 4] if 0 < tick < STREAMS else []
            following, hidden_stash, normed_stash = forward_step(
                tick, meta, received, firsts, gains, weights, hidden_stash, normed_stash, waits
            )
            if tick <= LAST:
                received = fan_out([following] * 4, forward_moves(tick))
            if tick == 4:
                tokens_0 = over_z(slot_rows(normed_stash, 0))
                after[5] = (tokens_0,)
            if tick == 5:
                tokens_0 = over_y(tokens_0)
                after[6] = tokens_0[1:]
            if tick == 6:
                picked_0 = picked_rows(tokens_0)
                after[7] = picked_0[1:]
            if tick == 8:
                tokens_1 = over_z(slot_rows(normed_stash, 1))
                after[9] = act_0[1:] + [tokens_1]
        if tick >= LAST:
            *sent, grad_stash = backward_step(
                tick, meta, last_deltas, back[0], back[1:], gains, weights, hidden_stash, grad_stash, waits
            )
            if tick < 2 * LAST + STREAMS - 1:
                back = fan_out(sent, backward_moves(tick))
            if tick == 7:
                act_0 = blocks_of(tokens_0, picked_0)
            if tick == 9:
                tokens_1 = over_y(tokens_1)
                after[10] = tokens_1[1:]
            if tick == 10:
                picked_1 = picked_rows(tokens_1)
                after[11] = picked_1[1:]
            if tick == 11:
                act_1 = blocks_of(tokens_1, picked_1)
                late = over_z(slot_rows(grad_stash, 1))
                after[12] = (late,)
            if tick == 12:
                late = over_y(late)
                after[13] = late[1:] + act_1[1:]
            if tick == 13:
                late_picked = picked_rows(late)
                after[14] = late_picked[1:]
            if tick == 14:
                grad_1 = blocks_of(late, late_picked)
                after[15] = grad_1[1:]
    act_factor = assemble(meta, act_0, act_1)
    early = over_y(over_z(slot_rows(grad_stash, 0)))
    grad_0 = blocks_of(early, picked_rows(early))
    grad_factor = assemble(meta, grad_0, grad_1)
    shape = (own_rows, 2, 1, features)
    return (act_factor.reshape(shape), grad_factor.reshape(shape))


def solution(mesh):
    split = Mesh(mesh.devices.reshape(SIZES), AXES)
    placed = (
        P(None, TENSOR_DP, None),
        P(None, "pipe", None, "tensor"),
        P(None, "pipe", None),
        P(None, TENSOR_DP, None),
    )
    return jax.shard_map(
        body,
        mesh=split,
        in_specs=placed,
        out_specs=(P(TENSOR_DP, None, "pipe", None), P(TENSOR_DP, None, "pipe", None)),
        check_vma=False,
    )
```

```python
import functools

import jax
import jax.numpy as jnp
from jax import lax
from jax.experimental import pallas as pl
from jax.experimental.pallas import tpu as pltpu
from jax.sharding import Mesh
from jax.sharding import PartitionSpec as P

DP = ("dp_0", "dp_1")
TENSOR_DP = ("tensor", "dp_0", "dp_1")
AXES = ("pipe", "tensor", "dp_0", "dp_1")
SIZES = (4, 4, 2, 4)
EPSILON = 1e-05
PIPES = 4
LAYERS = 8
LAST = LAYERS - 1
F32 = jnp.float32
BF16 = jnp.bfloat16
ANYWHERE = pl.BlockSpec(memory_space=pl.ANY)


def flat(place):
    index = 0
    for size, at in zip(SIZES, place):
        index = index * size + at
    return index


def permuted(array, target):
    pairs = []
    for pipe in range(SIZES[0]):
        for tensor in range(SIZES[1]):
            for z in range(SIZES[2]):
                for y in range(SIZES[3]):
                    there = target(pipe, tensor, z, y)
                    if there is not None:
                        pairs.append((flat((pipe, tensor, z, y)), flat(there)))
    return lax.ppermute(array, AXES, pairs)


def forward_moves(layer):
    return {0: {0: (1, 0), 2: (3, 0)}, 1: {1: (2, 1)}, 3: {3: (0, 1)}}[layer % PIPES if layer % 2 else 0]


def backward_moves(layer):
    return {1: {1: (0, 0), 3: (2, 0)}, 0: {0: (3, 1)}, 2: {2: (1, 1)}}[1 if layer % 2 else layer % PIPES]


def fan_out(arrays, moves):
    received = {}
    for step in (0, 1, 3, 2):

        def target(pipe, tensor, z, y, step=step):
            if pipe not in moves:
                return None
            there, flip = moves[pipe]
            return (there, (tensor + step) % SIZES[1], z ^ flip, y)

        received[step] = permuted(arrays[step], target)
    return [received[step] for step in range(4)]


def turned(index, count=4):
    return lax.rem(index + count, count)


def held(weights, after):
    pieces = 8
    rows = weights.shape[1] // pieces

    def kernel(source, *refs):
        target, sems = refs[-2:]
        copies = []
        for slot in range(weights.shape[0]):
            for k in range(pieces):
                part = pl.ds(k * rows, rows)
                copies.append(
                    pltpu.make_async_copy(
                        source.at[slot, part], target.at[slot, part], sems.at[slot, k]
                    )
                )
        for copy in copies:
            copy.start()
        for copy in copies:
            copy.wait()

    return pl.pallas_call(
        kernel,
        in_specs=[ANYWHERE] * (1 + len(after)),
        out_specs=pl.BlockSpec(memory_space=pltpu.VMEM),
        out_shape=pltpu.VMEM(weights.shape, weights.dtype),
        scratch_shapes=[pltpu.SemaphoreType.DMA((weights.shape[0], pieces))],
        compiler_params=pltpu.CompilerParams(vmem_limit_bytes=17 << 20),
        name="held",
    )(pltpu.with_memory_space_constraint(weights, pltpu.HBM), *after)


def ingest(meta, arrays):
    rows, features = arrays[0].shape
    half = rows // 2
    quarter = features // 4

    def kernel(meta_ref, *refs):
        sources, blocks, own_ref = refs[:4], refs[4:12], refs[12]
        tensor = meta_ref[1]
        for step in range(4):
            row = pl.multiple_of(turned(tensor - step) * half, half)
            for stream in range(2):
                for turn in range(4):
                    column = pl.multiple_of(turned(tensor - turn) * quarter, quarter)
                    piece = sources[step][stream * half : (stream + 1) * half, pl.ds(column, quarter)]
                    blocks[4 * stream + turn][pl.ds(row, half), :] = piece
                    if turn == 0:
                        own_ref[stream, pl.ds(row, half), :] = piece

    whole = pl.BlockSpec(memory_space=pltpu.VMEM)
    return pl.pallas_call(
        kernel,
        in_specs=[pl.BlockSpec(memory_space=pltpu.SMEM)] + [whole] * 4,
        out_specs=[whole] * 9,
        out_shape=[jax.ShapeDtypeStruct((4 * half, quarter), BF16)] * 8
        + [jax.ShapeDtypeStruct((2, 4 * half, quarter), BF16)],
        compiler_params=pltpu.CompilerParams(vmem_limit_bytes=8 << 20),
        name="ingest",
    )(meta, *arrays)


def ingest(meta, arrays):
    rows, features = arrays[0].shape
    quarter = features // 4

    def kernel(meta_ref, *refs):
        tensor = meta_ref[1]
        for step in range(4):
            row = pl.multiple_of(turned(tensor - step) * rows, rows)
            for turn in range(4):
                column = pl.multiple_of(turned(tensor - turn) * quarter, quarter)
                refs[4 + turn][pl.ds(row, rows), :] = refs[step][:, pl.ds(column, quarter)]

    whole = pl.BlockSpec(memory_space=pltpu.VMEM)
    return pl.pallas_call(
        kernel,
        in_specs=[pl.BlockSpec(memory_space=pltpu.SMEM)] + [whole] * 4,
        out_specs=[whole] * 4,
        out_shape=[jax.ShapeDtypeStruct((4 * rows, quarter), BF16)] * 4,
        compiler_params=pltpu.CompilerParams(vmem_limit_bytes=8 << 20),
        name="ingest",
    )(meta, *arrays)


def forward_step(layer, meta, blocks, gains, weights, stashes, after):
    rows, quarter = blocks[0].shape
    features = 4 * quarter
    pipe, slot, multiplies = layer % PIPES, layer // PIPES, layer < LAST

    def kernel(meta_ref, b0, b1, b2, b3, gain_ref, weight_ref, *refs):
        next_ref, hidden_ref, normed_ref, normed, total = refs[-5:]
        turn = pl.program_id(0)
        tensor = meta_ref[1]
        active = meta_ref[0] == pipe

        @pl.when(active & (turn == 0))
        def _():
            squares = 0.0
            for k, ref in enumerate((b0, b1, b2, b3)):
                hidden_ref[0, k] = ref[...]
                wide = ref[...].astype(F32)
                squares = squares + jnp.sum(wide * wide, axis=-1, keepdims=True)
            scale = lax.rsqrt(squares * (1.0 / features) + EPSILON)
            for k, ref in enumerate((b0, b1, b2, b3)):
                gain = gain_ref[slot, pl.ds(turned(tensor - k), 1), :]
                normed[k] = (ref[...].astype(F32) * scale * gain).astype(BF16)
            normed_ref[0] = normed[0]

        if multiplies:

            @pl.when(active)
            def _():
                part = jnp.dot(normed[turn], weight_ref[0], preferred_element_type=F32)

                @pl.when(turn == 0)
                def _():
                    total[...] = part

                @pl.when(turn > 0)
                def _():
                    total[...] += part

            @pl.when(active & (turn == 3))
            def _():
                rounded = total[...].astype(BF16).astype(F32)
                next_ref[...] = (b0[...].astype(F32) + rounded).astype(BF16)

    def weight_at(turn, meta_ref):
        return slot, jnp.where(meta_ref[0] == pipe, turned(meta_ref[1] - turn), 0), 0

    def stash_at(meta_ref):
        return jnp.where(meta_ref[0] == pipe, 0, 1)

    block = pl.BlockSpec((rows, quarter), lambda turn, meta_ref: (0, 0))
    return pl.pallas_call(
        kernel,
        grid_spec=pltpu.PrefetchScalarGridSpec(
            num_scalar_prefetch=1,
            grid=(4,),
            in_specs=[block] * 4
            + [
                pl.BlockSpec((2, 4, quarter), lambda turn, meta_ref: (0, 0, 0)),
                pl.BlockSpec((1, quarter, quarter), weight_at),
            ]
            + [ANYWHERE] * (len(stashes) + len(after)),
            out_specs=[
                block,
                pl.BlockSpec((1, 4, rows, quarter), lambda turn, m: (stash_at(m), 0, 0, 0)),
                pl.BlockSpec((1, rows, quarter), lambda turn, m: (stash_at(m), 0, 0)),
            ],
            scratch_shapes=[pltpu.VMEM((4, rows, quarter), BF16), pltpu.VMEM((rows, quarter), F32)],
        ),
        out_shape=[
            jax.ShapeDtypeStruct((rows, quarter), BF16),
            jax.ShapeDtypeStruct((2, 4, rows, quarter), BF16),
            jax.ShapeDtypeStruct((2, rows, quarter), BF16),
        ],
        input_output_aliases={7: 1, 8: 2} if stashes else {},
        compiler_params=pltpu.CompilerParams(vmem_limit_bytes=20 << 20),
        cost_estimate=pl.CostEstimate(
            flops=2 * rows * features * quarter, bytes_accessed=2 * features * quarter, transcendentals=0
        ),
        name="forward_step",
    )(meta, *blocks, gains, weights, *stashes, *after)


def backward_step(layer, meta, arrived, gains, weights, hidden_stash, stashes, after):
    rows, quarter = arrived[0].shape
    features = 4 * quarter
    pipe, slot, multiplies = layer % PIPES, layer // PIPES, layer > 0
    terms = len(arrived)

    def kernel(meta_ref, gain_ref, weight_ref, hidden_ref, *refs):
        own_out, o1, o2, o3, grad_ref, delta, scaled, inner = refs[-8:]
        turn = pl.program_id(0)
        tensor = meta_ref[1]
        active = meta_ref[0] == pipe

        @pl.when(active & (turn == 0))
        def _():
            total = refs[0][...].astype(F32)
            for ref in refs[1:terms]:
                total = total + ref[...].astype(F32)
            delta[...] = total.astype(BF16)
            grad_ref[0] = total.astype(BF16)

        if multiplies:

            @pl.when(active)
            def _():
                part = lax.dot_general(
                    delta[...], weight_ref[0], (((1,), (1,)), ((), ())), preferred_element_type=F32
                )
                gain = gain_ref[slot, pl.ds(turned(tensor + turn), 1), :]
                back = part.astype(BF16).astype(F32) * gain
                scaled[turn] = back
                hidden = hidden_ref[0, turned(-turn)].astype(F32)
                sums = jnp.broadcast_to(jnp.sum(hidden * back, axis=-1, keepdims=True), inner.shape)

                @pl.when(turn == 0)
                def _():
                    inner[...] = sums

                @pl.when(turn > 0)
                def _():
                    inner[...] += sums

            @pl.when(active & (turn == 3))
            def _():
                squares = 0.0
                for k in range(4):
                    wide = hidden_ref[0, k].astype(F32)
                    squares = squares + jnp.sum(wide * wide, axis=-1, keepdims=True)
                scale = lax.rsqrt(squares * (1.0 / features) + EPSILON)
                slope = scale * scale * scale * (inner[:, :1] * (1.0 / features))
                for k, ref in enumerate((own_out, o1, o2, o3)):
                    change = scale * scaled[k] - slope * hidden_ref[0, (4 - k) % 4].astype(F32)
                    if k == 0:
                        ref[...] = delta[...].astype(F32) + change
                    else:
                        ref[...] = change.astype(BF16)

    def weight_at(turn, meta_ref):
        return slot, jnp.where(meta_ref[0] == pipe, turned(meta_ref[1] + turn), 0), 0

    def stash_at(meta_ref):
        return jnp.where(meta_ref[0] == pipe, 0, 1)

    block = pl.BlockSpec((rows, quarter), lambda turn, meta_ref: (0, 0))
    return pl.pallas_call(
        kernel,
        grid_spec=pltpu.PrefetchScalarGridSpec(
            num_scalar_prefetch=1,
            grid=(4,),
            in_specs=[
                pl.BlockSpec((2, 4, quarter), lambda turn, meta_ref: (0, 0, 0)),
                pl.BlockSpec((1, quarter, quarter), weight_at),
                pl.BlockSpec((1, 4, rows, quarter), lambda turn, m: (0, 0, 0, 0)),
            ]
            + [block] * terms
            + [ANYWHERE] * (len(stashes) + len(after)),
            out_specs=[block] * 4 + [pl.BlockSpec((1, rows, quarter), lambda turn, m: (stash_at(m), 0, 0))],
            scratch_shapes=[
                pltpu.VMEM((rows, quarter), BF16),
                pltpu.VMEM((4, rows, quarter), F32),
                pltpu.VMEM((rows, 128), F32),
            ],
        ),
        out_shape=[jax.ShapeDtypeStruct((rows, quarter), F32)]
        + [jax.ShapeDtypeStruct((rows, quarter), BF16)] * 3
        + [jax.ShapeDtypeStruct((2, rows, quarter), BF16)],
        input_output_aliases={4 + terms: 4} if stashes else {},
        compiler_params=pltpu.CompilerParams(vmem_limit_bytes=20 << 20),
        cost_estimate=pl.CostEstimate(
            flops=2 * rows * features * quarter, bytes_accessed=2 * features * quarter, transcendentals=0
        ),
        name="backward_step",
    )(meta, gains, weights, hidden_stash, *arrived, *stashes, *after)


def joined(first, second, after):
    rows, columns = first.shape

    def kernel(a_ref, b_ref, *refs):
        refs[-1][:rows, :] = a_ref[...]
        refs[-1][rows:, :] = b_ref[...]

    whole = pl.BlockSpec(memory_space=pltpu.VMEM)
    return pl.pallas_call(
        kernel,
        in_specs=[whole] * 2 + [ANYWHERE] * len(after),
        out_specs=whole,
        out_shape=jax.ShapeDtypeStruct((2 * rows, columns), first.dtype),
        compiler_params=pltpu.CompilerParams(vmem_limit_bytes=8 << 20),
        name="joined",
    )(first, second, *after)


def own_columns(meta, pieces, own, after):
    rows = pieces[0].shape[0]

    def kernel(meta_ref, *refs):
        column = pl.multiple_of(meta_ref[2] * own, own)
        for k, piece in enumerate(refs[: len(pieces)]):
            refs[-1][k * rows : (k + 1) * rows, :] = piece[:, pl.ds(column, own)]

    whole = pl.BlockSpec(memory_space=pltpu.VMEM)
    return pl.pallas_call(
        kernel,
        in_specs=[pl.BlockSpec(memory_space=pltpu.SMEM)] + [whole] * len(pieces) + [ANYWHERE] * len(after),
        out_specs=whole,
        out_shape=jax.ShapeDtypeStruct((rows * len(pieces), own), BF16),
        compiler_params=pltpu.CompilerParams(vmem_limit_bytes=8 << 20),
        name="own_columns",
    )(meta, *pieces, *after)


def gram(pieces, picked, inv_tokens, after):
    quarter = pieces[0].shape[-1]
    count, own = picked[0].shape
    starts = [0]
    for piece in pieces:
        starts.append(starts[-1] + piece.shape[0])

    def kernel(*refs):
        token_refs, picked_refs, outs = refs[: len(pieces)], refs[len(pieces) : len(pieces) + 4], refs[-4:]
        for left, out in zip(picked_refs, outs):
            product = 0.0
            for ref, start, stop in zip(token_refs, starts, starts[1:]):
                product = product + lax.dot_general(
                    left[start:stop, :], ref[...], (((0,), (0,)), ((), ())), preferred_element_type=F32
                )
            out[...] = (product * inv_tokens).astype(BF16)

    whole = pl.BlockSpec(memory_space=pltpu.VMEM)
    return pl.pallas_call(
        kernel,
        in_specs=[whole] * (len(pieces) + 4) + [ANYWHERE] * len(after),
        out_specs=[whole] * 4,
        out_shape=[jax.ShapeDtypeStruct((own, quarter), BF16)] * 4,
        compiler_params=pltpu.CompilerParams(vmem_limit_bytes=20 << 20),
        cost_estimate=pl.CostEstimate(
            flops=2 * count * 4 * own * quarter,
            bytes_accessed=2 * (count * quarter + 8 * own * quarter),
            transcendentals=0,
        ),
        name="gram",
    )(*pieces, *picked, *after)


def shifted(array, x=0, y=0, z=0):
    return permuted(array, lambda p, t, u, v: (p, (t + x) % SIZES[1], u ^ z, (v + y) % SIZES[3]))


def share_columns(blocks):
    return [blocks[0]] + [shifted(blocks[4 - k], x=k) for k in (1, 2, 3)]


def assemble(meta, first, second, after):
    own, quarter = first[0].shape

    def kernel(meta_ref, *refs):
        out = refs[-1]
        tensor = meta_ref[1]
        for step in range(4):
            column = pl.multiple_of(turned(tensor - step) * quarter, quarter)
            out[:, :, pl.ds(column, quarter)] = jnp.stack([refs[step][...], refs[4 + step][...]], 1)

    whole = pl.BlockSpec(memory_space=pltpu.VMEM)
    return pl.pallas_call(
        kernel,
        in_specs=[pl.BlockSpec(memory_space=pltpu.SMEM)] + [whole] * 8 + [ANYWHERE] * len(after),
        out_specs=whole,
        out_shape=jax.ShapeDtypeStruct((own, 2, 4 * quarter), BF16),
        compiler_params=pltpu.CompilerParams(vmem_limit_bytes=20 << 20),
        name="assemble",
    )(meta, *first, *second, *after)


def body(inputs, weights, norm_gains, cotangent):
    micro_count, shard_rows, features = inputs.shape
    quarter = weights.shape[3]
    pipe = lax.axis_index("pipe")
    tensor = lax.axis_index("tensor")
    group = lax.axis_index(DP)
    own_rows = quarter // lax.axis_size(DP)
    inv_tokens = 1.0 / (micro_count * shard_rows * lax.axis_size(TENSOR_DP))
    meta = jnp.stack([pipe, tensor, group]).astype(jnp.int32)
    gains = norm_gains.reshape(norm_gains.shape[0], 4, quarter)
    weights = held(weights.reshape(weights.shape[0], features, quarter), (meta, gains))
    weights = pltpu.with_memory_space_constraint(weights, pltpu.VMEM)

    given = jnp.where(pipe == LAST % PIPES, cotangent, inputs).reshape(-1, features)
    received = ingest(meta, [given] + [shifted(given, x=k) for k in (1, 2, 3)])
    back = [shifted(received[0], z=1)]

    def over_y(rows, other, after):
        both = joined(rows, other, after)
        return [both] + [shifted(both, y=k) for k in (1, 2, 3)]

    def over_x(mine):
        return [mine] + [shifted(mine, x=k) for k in (1, 2, 3)]

    def blocks_of(pieces, picked, after):
        return share_columns(gram(pieces, picked, inv_tokens, after))

    hidden, normed, grads = {}, {}, {}
    rows, other, pieces, blocks = {}, {}, {}, {}
    due = {tick: [] for tick in range(2 * LAST + 4)}
    due[2] += back
    over_z_at = {3: "act_0", 7: "act_1", 10: "grad_1"}
    over_y_at = {4: "act_0", 8: "act_1", 11: "grad_1"}
    for tick in range(2 * LAST + 1):
        waits = due[tick]
        if tick <= LAST:
            slot = tick // PIPES
            stashes = [hidden[slot], normed[slot]] if slot in hidden else []
            following, hidden[slot], normed[slot] = forward_step(
                tick, meta, received, gains, weights, stashes, waits
            )
            if tick < LAST:
                received = fan_out([following] * 4, forward_moves(tick))
                arrived = received[:1]
        if tick >= LAST:
            layer = 2 * LAST - tick
            slot = layer // PIPES
            stashes = [grads[slot]] if slot in grads else []
            *sent, grads[slot] = backward_step(
                layer, meta, back, gains, weights, hidden[slot], stashes, waits
            )
            if layer:
                back = fan_out(sent, backward_moves(layer))
                arrived = back[:1]
        if tick in over_z_at:
            name = over_z_at[tick]
            rows[name] = {"act_0": normed, "act_1": normed, "grad_1": grads}[name][int(name[-1])][0]
            other[name] = shifted(rows[name], z=1)
            due[tick + 1] += [other[name]]
        if tick in over_y_at:
            name = over_y_at[tick]
            pieces[name] = over_y(rows[name], other[name], arrived)
            for later, piece in enumerate(pieces[name][1:]):
                due[tick + 1 + later].append(piece)
    rows["grad_0"] = grads[0][0]
    other["grad_0"] = shifted(rows["grad_0"], z=1)
    pieces["grad_0"] = over_y(rows["grad_0"], other["grad_0"], [])
    for name in ("act_0", "act_1", "grad_1", "grad_0"):
        picked = over_x(own_columns(meta, pieces[name], own_rows, [rows["grad_0"]]))
        blocks[name] = blocks_of(pieces[name], picked, [])
    act_factor = assemble(meta, blocks["act_0"], blocks["act_1"], [])
    grad_factor = assemble(meta, blocks["grad_0"], blocks["grad_1"], [])
    shape = (own_rows, 2, 1, features)
    return (act_factor.reshape(shape), grad_factor.reshape(shape))


def solution(mesh):
    split = Mesh(mesh.devices.reshape(SIZES), AXES)
    placed = (
        P(None, TENSOR_DP, None),
        P(None, "pipe", None, "tensor"),
        P(None, "pipe", None),
        P(None, TENSOR_DP, None),
    )
    return jax.shard_map(
        body,
        mesh=split,
        in_specs=placed,
        out_specs=(P(TENSOR_DP, None, "pipe", None), P(TENSOR_DP, None, "pipe", None)),
        check_vma=False,
    )
```

```python
import functools

import jax
import jax.numpy as jnp
from jax import lax
from jax.experimental import pallas as pl
from jax.experimental.pallas import tpu as pltpu
from jax.sharding import Mesh
from jax.sharding import PartitionSpec as P

DP = ("dp_0", "dp_1")
TENSOR_DP = ("tensor", "dp_0", "dp_1")
AXES = ("pipe", "tensor", "dp_0", "dp_1")
SIZES = (4, 4, 2, 4)
EPSILON = 1e-05
PIPES = 4
LAYERS = 8
LAST = LAYERS - 1
F32 = jnp.float32
BF16 = jnp.bfloat16
ANYWHERE = pl.BlockSpec(memory_space=pl.ANY)


def flat(place):
    index = 0
    for size, at in zip(SIZES, place):
        index = index * size + at
    return index


def permuted(array, target):
    pairs = []
    for pipe in range(SIZES[0]):
        for tensor in range(SIZES[1]):
            for z in range(SIZES[2]):
                for y in range(SIZES[3]):
                    there = target(pipe, tensor, z, y)
                    if there is not None:
                        pairs.append((flat((pipe, tensor, z, y)), flat(there)))
    return lax.ppermute(array, AXES, pairs)


def forward_moves(layer):
    return {0: {0: (1, 0), 2: (3, 0)}, 1: {1: (2, 1)}, 3: {3: (0, 1)}}[layer % PIPES if layer % 2 else 0]


def backward_moves(layer):
    return {1: {1: (0, 0), 3: (2, 0)}, 0: {0: (3, 1)}, 2: {2: (1, 1)}}[1 if layer % 2 else layer % PIPES]


def fan_out(arrays, moves):
    received = {}
    for step in (0, 1, 3, 2):

        def target(pipe, tensor, z, y, step=step):
            if pipe not in moves:
                return None
            there, flip = moves[pipe]
            return (there, (tensor + step) % SIZES[1], z ^ flip, y)

        received[step] = permuted(arrays[step], target)
    return [received[step] for step in range(4)]


def turned(index, count=4):
    return lax.rem(index + count, count)


def held(weights, after):
    pieces = 8
    rows = weights.shape[1] // pieces

    def kernel(source, *refs):
        target, sems = refs[-2:]
        copies = []
        for slot in range(weights.shape[0]):
            for k in range(pieces):
                part = pl.ds(k * rows, rows)
                copies.append(
                    pltpu.make_async_copy(
                        source.at[slot, part], target.at[slot, part], sems.at[slot, k]
                    )
                )
        for copy in copies:
            copy.start()
        for copy in copies:
            copy.wait()

    return pl.pallas_call(
        kernel,
        in_specs=[ANYWHERE] * (1 + len(after)),
        out_specs=pl.BlockSpec(memory_space=pltpu.VMEM),
        out_shape=pltpu.VMEM(weights.shape, weights.dtype),
        scratch_shapes=[pltpu.SemaphoreType.DMA((weights.shape[0], pieces))],
        compiler_params=pltpu.CompilerParams(vmem_limit_bytes=17 << 20),
        name="held",
    )(pltpu.with_memory_space_constraint(weights, pltpu.HBM), *after)


def ingest(meta, arrays):
    rows, features = arrays[0].shape
    half = rows // 2
    quarter = features // 4

    def kernel(meta_ref, *refs):
        sources, blocks, own_ref = refs[:4], refs[4:12], refs[12]
        tensor = meta_ref[1]
        for step in range(4):
            row = pl.multiple_of(turned(tensor - step) * half, half)
            for stream in range(2):
                for turn in range(4):
                    column = pl.multiple_of(turned(tensor - turn) * quarter, quarter)
                    piece = sources[step][stream * half : (stream + 1) * half, pl.ds(column, quarter)]
                    blocks[4 * stream + turn][pl.ds(row, half), :] = piece
                    if turn == 0:
                        own_ref[stream, pl.ds(row, half), :] = piece

    whole = pl.BlockSpec(memory_space=pltpu.VMEM)
    return pl.pallas_call(
        kernel,
        in_specs=[pl.BlockSpec(memory_space=pltpu.SMEM)] + [whole] * 4,
        out_specs=[whole] * 9,
        out_shape=[jax.ShapeDtypeStruct((4 * half, quarter), BF16)] * 8
        + [jax.ShapeDtypeStruct((2, 4 * half, quarter), BF16)],
        compiler_params=pltpu.CompilerParams(vmem_limit_bytes=8 << 20),
        name="ingest",
    )(meta, *arrays)


def ingest(meta, arrays):
    rows, features = arrays[0].shape
    quarter = features // 4

    def kernel(meta_ref, *refs):
        tensor = meta_ref[1]
        for step in range(4):
            row = pl.multiple_of(turned(tensor - step) * rows, rows)
            for turn in range(4):
                column = pl.multiple_of(turned(tensor - turn) * quarter, quarter)
                refs[4 + turn][pl.ds(row, rows), :] = refs[step][:, pl.ds(column, quarter)]

    whole = pl.BlockSpec(memory_space=pltpu.VMEM)
    return pl.pallas_call(
        kernel,
        in_specs=[pl.BlockSpec(memory_space=pltpu.SMEM)] + [whole] * 4,
        out_specs=[whole] * 4,
        out_shape=[jax.ShapeDtypeStruct((4 * rows, quarter), BF16)] * 4,
        compiler_params=pltpu.CompilerParams(vmem_limit_bytes=8 << 20),
        name="ingest",
    )(meta, *arrays)


def forward_step(layer, meta, blocks, gains, weights, stashes, after):
    rows, quarter = blocks[0].shape
    features = 4 * quarter
    pipe, slot, multiplies = layer % PIPES, layer // PIPES, layer < LAST

    def kernel(meta_ref, b0, b1, b2, b3, gain_ref, weight_ref, *refs):
        next_ref, hidden_ref, normed_ref, normed, total = refs[-5:]
        turn = pl.program_id(0)
        tensor = meta_ref[1]
        active = meta_ref[0] == pipe

        @pl.when(active & (turn == 0))
        def _():
            squares = 0.0
            for k, ref in enumerate((b0, b1, b2, b3)):
                hidden_ref[0, k] = ref[...]
                wide = ref[...].astype(F32)
                squares = squares + jnp.sum(wide * wide, axis=-1, keepdims=True)
            scale = lax.rsqrt(squares * (1.0 / features) + EPSILON)
            for k, ref in enumerate((b0, b1, b2, b3)):
                gain = gain_ref[slot, pl.ds(turned(tensor - k), 1), :]
                normed[k] = (ref[...].astype(F32) * scale * gain).astype(BF16)
            normed_ref[0] = normed[0]

        if multiplies:

            @pl.when(active)
            def _():
                part = jnp.dot(normed[turn], weight_ref[0], preferred_element_type=F32)

                @pl.when(turn == 0)
                def _():
                    total[...] = part

                @pl.when(turn > 0)
                def _():
                    total[...] += part

            @pl.when(active & (turn == 3))
            def _():
                rounded = total[...].astype(BF16).astype(F32)
                next_ref[...] = (b0[...].astype(F32) + rounded).astype(BF16)

    def weight_at(turn, meta_ref):
        return slot, jnp.where(meta_ref[0] == pipe, turned(meta_ref[1] - turn), 0), 0

    def stash_at(meta_ref):
        return jnp.where(meta_ref[0] == pipe, 0, 1)

    block = pl.BlockSpec((rows, quarter), lambda turn, meta_ref: (0, 0))
    return pl.pallas_call(
        kernel,
        grid_spec=pltpu.PrefetchScalarGridSpec(
            num_scalar_prefetch=1,
            grid=(4,),
            in_specs=[block] * 4
            + [
                pl.BlockSpec((2, 4, quarter), lambda turn, meta_ref: (0, 0, 0)),
                pl.BlockSpec((1, quarter, quarter), weight_at),
            ]
            + [ANYWHERE] * (len(stashes) + len(after)),
            out_specs=[
                block,
                pl.BlockSpec((1, 4, rows, quarter), lambda turn, m: (stash_at(m), 0, 0, 0)),
                pl.BlockSpec((1, rows, quarter), lambda turn, m: (stash_at(m), 0, 0)),
            ],
            scratch_shapes=[pltpu.VMEM((4, rows, quarter), BF16), pltpu.VMEM((rows, quarter), F32)],
        ),
        out_shape=[
            jax.ShapeDtypeStruct((rows, quarter), BF16),
            jax.ShapeDtypeStruct((2, 4, rows, quarter), BF16),
            jax.ShapeDtypeStruct((2, rows, quarter), BF16),
        ],
        input_output_aliases={7: 1, 8: 2} if stashes else {},
        compiler_params=pltpu.CompilerParams(vmem_limit_bytes=20 << 20),
        cost_estimate=pl.CostEstimate(
            flops=2 * rows * features * quarter, bytes_accessed=2 * features * quarter, transcendentals=0
        ),
        name="forward_step",
    )(meta, *blocks, gains, weights, *stashes, *after)


def backward_step(layer, meta, arrived, gains, weights, hidden_stash, stashes, after):
    rows, quarter = arrived[0].shape
    features = 4 * quarter
    pipe, slot, multiplies = layer % PIPES, layer // PIPES, layer > 0
    terms = len(arrived)

    def kernel(meta_ref, gain_ref, weight_ref, hidden_ref, *refs):
        own_out, o1, o2, o3, grad_ref, delta, scaled, inner = refs[-8:]
        turn = pl.program_id(0)
        tensor = meta_ref[1]
        active = meta_ref[0] == pipe

        @pl.when(active & (turn == 0))
        def _():
            total = refs[0][...].astype(F32)
            for ref in refs[1:terms]:
                total = total + ref[...].astype(F32)
            delta[...] = total.astype(BF16)
            grad_ref[0] = total.astype(BF16)

        if multiplies:

            @pl.when(active)
            def _():
                part = lax.dot_general(
                    delta[...], weight_ref[0], (((1,), (1,)), ((), ())), preferred_element_type=F32
                )
                gain = gain_ref[slot, pl.ds(turned(tensor + turn), 1), :]
                back = part.astype(BF16).astype(F32) * gain
                scaled[turn] = back
                hidden = hidden_ref[0, turned(-turn)].astype(F32)
                sums = jnp.broadcast_to(jnp.sum(hidden * back, axis=-1, keepdims=True), inner.shape)

                @pl.when(turn == 0)
                def _():
                    inner[...] = sums

                @pl.when(turn > 0)
                def _():
                    inner[...] += sums

            @pl.when(active & (turn == 3))
            def _():
                squares = 0.0
                for k in range(4):
                    wide = hidden_ref[0, k].astype(F32)
                    squares = squares + jnp.sum(wide * wide, axis=-1, keepdims=True)
                scale = lax.rsqrt(squares * (1.0 / features) + EPSILON)
                slope = scale * scale * scale * (inner[:, :1] * (1.0 / features))
                for k, ref in enumerate((own_out, o1, o2, o3)):
                    change = scale * scaled[k] - slope * hidden_ref[0, (4 - k) % 4].astype(F32)
                    if k == 0:
                        ref[...] = delta[...].astype(F32) + change
                    else:
                        ref[...] = change.astype(BF16)

    def weight_at(turn, meta_ref):
        return slot, jnp.where(meta_ref[0] == pipe, turned(meta_ref[1] + turn), 0), 0

    def stash_at(meta_ref):
        return jnp.where(meta_ref[0] == pipe, 0, 1)

    block = pl.BlockSpec((rows, quarter), lambda turn, meta_ref: (0, 0))
    return pl.pallas_call(
        kernel,
        grid_spec=pltpu.PrefetchScalarGridSpec(
            num_scalar_prefetch=1,
            grid=(4,),
            in_specs=[
                pl.BlockSpec((2, 4, quarter), lambda turn, meta_ref: (0, 0, 0)),
                pl.BlockSpec((1, quarter, quarter), weight_at),
                pl.BlockSpec((1, 4, rows, quarter), lambda turn, m: (0, 0, 0, 0)),
            ]
            + [block] * terms
            + [ANYWHERE] * (len(stashes) + len(after)),
            out_specs=[block] * 4 + [pl.BlockSpec((1, rows, quarter), lambda turn, m: (stash_at(m), 0, 0))],
            scratch_shapes=[
                pltpu.VMEM((rows, quarter), BF16),
                pltpu.VMEM((4, rows, quarter), F32),
                pltpu.VMEM((rows, 128), F32),
            ],
        ),
        out_shape=[jax.ShapeDtypeStruct((rows, quarter), F32)]
        + [jax.ShapeDtypeStruct((rows, quarter), BF16)] * 3
        + [jax.ShapeDtypeStruct((2, rows, quarter), BF16)],
        input_output_aliases={4 + terms: 4} if stashes else {},
        compiler_params=pltpu.CompilerParams(vmem_limit_bytes=20 << 20),
        cost_estimate=pl.CostEstimate(
            flops=2 * rows * features * quarter, bytes_accessed=2 * features * quarter, transcendentals=0
        ),
        name="backward_step",
    )(meta, gains, weights, hidden_stash, *arrived, *stashes, *after)


def joined(first, second, after):
    rows, columns = first.shape

    def kernel(a_ref, b_ref, *refs):
        refs[-1][:rows, :] = a_ref[...]
        refs[-1][rows:, :] = b_ref[...]

    whole = pl.BlockSpec(memory_space=pltpu.VMEM)
    return pl.pallas_call(
        kernel,
        in_specs=[whole] * 2 + [ANYWHERE] * len(after),
        out_specs=whole,
        out_shape=jax.ShapeDtypeStruct((2 * rows, columns), first.dtype),
        compiler_params=pltpu.CompilerParams(vmem_limit_bytes=8 << 20),
        name="joined",
    )(first, second, *after)


def own_columns(meta, pieces, own, after):
    rows = pieces[0].shape[0]

    def kernel(meta_ref, *refs):
        column = pl.multiple_of(meta_ref[2] * own, own)
        for k, piece in enumerate(refs[: len(pieces)]):
            refs[-1][k * rows : (k + 1) * rows, :] = piece[:, pl.ds(column, own)]

    whole = pl.BlockSpec(memory_space=pltpu.VMEM)
    return pl.pallas_call(
        kernel,
        in_specs=[pl.BlockSpec(memory_space=pltpu.SMEM)] + [whole] * len(pieces) + [ANYWHERE] * len(after),
        out_specs=whole,
        out_shape=jax.ShapeDtypeStruct((rows * len(pieces), own), BF16),
        compiler_params=pltpu.CompilerParams(vmem_limit_bytes=8 << 20),
        name="own_columns",
    )(meta, *pieces, *after)


def gram(pieces, picked, inv_tokens, after):
    quarter = pieces[0].shape[-1]
    count, own = picked[0].shape
    starts = [0]
    for piece in pieces:
        starts.append(starts[-1] + piece.shape[0])

    def kernel(*refs):
        token_refs, picked_refs, outs = refs[: len(pieces)], refs[len(pieces) : len(pieces) + 4], refs[-4:]
        for left, out in zip(picked_refs, outs):
            product = 0.0
            for ref, start, stop in zip(token_refs, starts, starts[1:]):
                product = product + lax.dot_general(
                    left[start:stop, :], ref[...], (((0,), (0,)), ((), ())), preferred_element_type=F32
                )
            out[...] = (product * inv_tokens).astype(BF16)

    whole = pl.BlockSpec(memory_space=pltpu.VMEM)
    return pl.pallas_call(
        kernel,
        in_specs=[whole] * (len(pieces) + 4) + [ANYWHERE] * len(after),
        out_specs=[whole] * 4,
        out_shape=[jax.ShapeDtypeStruct((own, quarter), BF16)] * 4,
        compiler_params=pltpu.CompilerParams(vmem_limit_bytes=20 << 20),
        cost_estimate=pl.CostEstimate(
            flops=2 * count * 4 * own * quarter,
            bytes_accessed=2 * (count * quarter + 8 * own * quarter),
            transcendentals=0,
        ),
        name="gram",
    )(*pieces, *picked, *after)


def shifted(array, x=0, y=0, z=0):
    return permuted(array, lambda p, t, u, v: (p, (t + x) % SIZES[1], u ^ z, (v + y) % SIZES[3]))


def share_columns(blocks):
    return [blocks[0]] + [shifted(blocks[4 - k], x=k) for k in (1, 2, 3)]


def assemble(meta, first, second, after):
    own, quarter = first[0].shape

    def kernel(meta_ref, *refs):
        out = refs[-1]
        tensor = meta_ref[1]
        for step in range(4):
            column = pl.multiple_of(turned(tensor - step) * quarter, quarter)
            out[:, :, pl.ds(column, quarter)] = jnp.stack([refs[step][...], refs[4 + step][...]], 1)

    whole = pl.BlockSpec(memory_space=pltpu.VMEM)
    return pl.pallas_call(
        kernel,
        in_specs=[pl.BlockSpec(memory_space=pltpu.SMEM)] + [whole] * 8 + [ANYWHERE] * len(after),
        out_specs=whole,
        out_shape=jax.ShapeDtypeStruct((own, 2, 4 * quarter), BF16),
        compiler_params=pltpu.CompilerParams(vmem_limit_bytes=20 << 20),
        name="assemble",
    )(meta, *first, *second, *after)


def body(inputs, weights, norm_gains, cotangent):
    micro_count, shard_rows, features = inputs.shape
    quarter = weights.shape[3]
    pipe = lax.axis_index("pipe")
    tensor = lax.axis_index("tensor")
    group = lax.axis_index(DP)
    own_rows = quarter // lax.axis_size(DP)
    inv_tokens = 1.0 / (micro_count * shard_rows * lax.axis_size(TENSOR_DP))
    meta = jnp.stack([pipe, tensor, group]).astype(jnp.int32)
    gains = norm_gains.reshape(norm_gains.shape[0], 4, quarter)
    weights = held(weights.reshape(weights.shape[0], features, quarter), (meta, gains))
    weights = pltpu.with_memory_space_constraint(weights, pltpu.VMEM)

    given = jnp.where(pipe == LAST % PIPES, cotangent, inputs).reshape(-1, features)
    received = ingest(meta, [given] + [shifted(given, x=k) for k in (1, 2, 3)])
    back = [shifted(received[0], z=1)]

    def over_y(rows, other, after):
        both = joined(rows, other, after)
        return [both] + [shifted(both, y=k) for k in (1, 2, 3)]

    def over_x(mine):
        return [mine] + [shifted(mine, x=k) for k in (1, 2, 3)]

    def blocks_of(pieces, picked, after):
        return share_columns(gram(pieces, picked, inv_tokens, after))

    hidden, normed, grads = {}, {}, {}
    rows, other, pieces, picked, blocks = {}, {}, {}, {}, {}
    due = {tick: [] for tick in range(2 * LAST + 4)}
    due[2] += back
    over_z_at = {3: "act_0", 7: "act_1", 10: "grad_1"}
    over_y_at = {4: "act_0", 8: "act_1", 11: "grad_1"}
    for tick in range(2 * LAST + 1):
        waits = due[tick]
        if tick <= LAST:
            slot = tick // PIPES
            stashes = [hidden[slot], normed[slot]] if slot in hidden else []
            following, hidden[slot], normed[slot] = forward_step(
                tick, meta, received, gains, weights, stashes, waits
            )
            if tick < LAST:
                received = fan_out([following] * 4, forward_moves(tick))
                arrived = received[:1]
        if tick >= LAST:
            layer = 2 * LAST - tick
            slot = layer // PIPES
            stashes = [grads[slot]] if slot in grads else []
            *sent, grads[slot] = backward_step(
                layer, meta, back, gains, weights, hidden[slot], stashes, waits
            )
            if layer:
                back = fan_out(sent, backward_moves(layer))
                arrived = back[:1]
        if tick in over_z_at:
            name = over_z_at[tick]
            rows[name] = {"act_0": normed, "act_1": normed, "grad_1": grads}[name][int(name[-1])][0]
            other[name] = shifted(rows[name], z=1)
            due[tick + 1] += [other[name]]
        if tick in over_y_at:
            name = over_y_at[tick]
            pieces[name] = over_y(rows[name], other[name], arrived)
            for later, piece in enumerate(pieces[name][1:]):
                due[tick + 1 + later].append(piece)
        if tick == 9:
            picked["act_0"] = over_x(own_columns(meta, pieces["act_0"], own_rows, arrived))
            due[11] += picked["act_0"][1:]
        if tick == 12:
            picked["act_1"] = over_x(own_columns(meta, pieces["act_1"], own_rows, arrived))
        if tick == 13:
            blocks["act_0"] = blocks_of(pieces["act_0"], picked["act_0"], arrived)
    rows["grad_0"] = grads[0][0]
    other["grad_0"] = shifted(rows["grad_0"], z=1)
    pieces["grad_0"] = over_y(rows["grad_0"], other["grad_0"], [])
    for name in ("grad_1", "grad_0"):
        picked[name] = over_x(own_columns(meta, pieces[name], own_rows, [rows["grad_0"]]))
    for name in ("act_1", "grad_1", "grad_0"):
        blocks[name] = blocks_of(pieces[name], picked[name], [rows["grad_0"]])
    act_factor = assemble(meta, blocks["act_0"], blocks["act_1"], [])
    grad_factor = assemble(meta, blocks["grad_0"], blocks["grad_1"], [])
    shape = (own_rows, 2, 1, features)
    return (act_factor.reshape(shape), grad_factor.reshape(shape))


def solution(mesh):
    split = Mesh(mesh.devices.reshape(SIZES), AXES)
    placed = (
        P(None, TENSOR_DP, None),
        P(None, "pipe", None, "tensor"),
        P(None, "pipe", None),
        P(None, TENSOR_DP, None),
    )
    return jax.shard_map(
        body,
        mesh=split,
        in_specs=placed,
        out_specs=(P(TENSOR_DP, None, "pipe", None), P(TENSOR_DP, None, "pipe", None)),
        check_vma=False,
    )
```

```python
import functools

import jax
import jax.numpy as jnp
from jax import lax
from jax.experimental import pallas as pl
from jax.experimental.pallas import tpu as pltpu
from jax.sharding import Mesh
from jax.sharding import PartitionSpec as P

DP = ("dp_0", "dp_1")
TENSOR_DP = ("tensor", "dp_0", "dp_1")
AXES = ("pipe", "tensor", "dp_0", "dp_1")
SIZES = (4, 4, 2, 4)
EPSILON = 1e-05
PIPES = 4
LAYERS = 8
LAST = LAYERS - 1
F32 = jnp.float32
BF16 = jnp.bfloat16
ANYWHERE = pl.BlockSpec(memory_space=pl.ANY)


def flat(place):
    index = 0
    for size, at in zip(SIZES, place):
        index = index * size + at
    return index


def permuted(array, target):
    pairs = []
    for pipe in range(SIZES[0]):
        for tensor in range(SIZES[1]):
            for z in range(SIZES[2]):
                for y in range(SIZES[3]):
                    there = target(pipe, tensor, z, y)
                    if there is not None:
                        pairs.append((flat((pipe, tensor, z, y)), flat(there)))
    return lax.ppermute(array, AXES, pairs)


def forward_moves(layer):
    return {0: {0: (1, 0), 2: (3, 0)}, 1: {1: (2, 1)}, 3: {3: (0, 1)}}[layer % PIPES if layer % 2 else 0]


def backward_moves(layer):
    return {1: {1: (0, 0), 3: (2, 0)}, 0: {0: (3, 1)}, 2: {2: (1, 1)}}[1 if layer % 2 else layer % PIPES]


def fan_out(arrays, moves):
    received = {}
    for step in (0, 1, 3, 2):

        def target(pipe, tensor, z, y, step=step):
            if pipe not in moves:
                return None
            there, flip = moves[pipe]
            return (there, (tensor + step) % SIZES[1], z ^ flip, y)

        received[step] = permuted(arrays[step], target)
    return [received[step] for step in range(4)]


def turned(index, count=4):
    return lax.rem(index + count, count)


def held(weights, after):
    pieces = 8
    rows = weights.shape[1] // pieces

    def kernel(source, *refs):
        target, sems = refs[-2:]
        copies = []
        for slot in range(weights.shape[0]):
            for k in range(pieces):
                part = pl.ds(k * rows, rows)
                copies.append(
                    pltpu.make_async_copy(
                        source.at[slot, part], target.at[slot, part], sems.at[slot, k]
                    )
                )
        for copy in copies:
            copy.start()
        for copy in copies:
            copy.wait()

    return pl.pallas_call(
        kernel,
        in_specs=[ANYWHERE] * (1 + len(after)),
        out_specs=pl.BlockSpec(memory_space=pltpu.VMEM),
        out_shape=pltpu.VMEM(weights.shape, weights.dtype),
        scratch_shapes=[pltpu.SemaphoreType.DMA((weights.shape[0], pieces))],
        compiler_params=pltpu.CompilerParams(vmem_limit_bytes=17 << 20),
        name="held",
    )(pltpu.with_memory_space_constraint(weights, pltpu.HBM), *after)


def ingest(meta, arrays):
    rows, features = arrays[0].shape
    half = rows // 2
    quarter = features // 4

    def kernel(meta_ref, *refs):
        sources, blocks, own_ref = refs[:4], refs[4:12], refs[12]
        tensor = meta_ref[1]
        for step in range(4):
            row = pl.multiple_of(turned(tensor - step) * half, half)
            for stream in range(2):
                for turn in range(4):
                    column = pl.multiple_of(turned(tensor - turn) * quarter, quarter)
                    piece = sources[step][stream * half : (stream + 1) * half, pl.ds(column, quarter)]
                    blocks[4 * stream + turn][pl.ds(row, half), :] = piece
                    if turn == 0:
                        own_ref[stream, pl.ds(row, half), :] = piece

    whole = pl.BlockSpec(memory_space=pltpu.VMEM)
    return pl.pallas_call(
        kernel,
        in_specs=[pl.BlockSpec(memory_space=pltpu.SMEM)] + [whole] * 4,
        out_specs=[whole] * 9,
        out_shape=[jax.ShapeDtypeStruct((4 * half, quarter), BF16)] * 8
        + [jax.ShapeDtypeStruct((2, 4 * half, quarter), BF16)],
        compiler_params=pltpu.CompilerParams(vmem_limit_bytes=8 << 20),
        name="ingest",
    )(meta, *arrays)


def ingest(meta, arrays):
    rows, features = arrays[0].shape
    quarter = features // 4

    def kernel(meta_ref, *refs):
        tensor = meta_ref[1]
        for step in range(4):
            row = pl.multiple_of(turned(tensor - step) * rows, rows)
            for turn in range(4):
                column = pl.multiple_of(turned(tensor - turn) * quarter, quarter)
                refs[4 + turn][pl.ds(row, rows), :] = refs[step][:, pl.ds(column, quarter)]

    whole = pl.BlockSpec(memory_space=pltpu.VMEM)
    return pl.pallas_call(
        kernel,
        in_specs=[pl.BlockSpec(memory_space=pltpu.SMEM)] + [whole] * 4,
        out_specs=[whole] * 4,
        out_shape=[jax.ShapeDtypeStruct((4 * rows, quarter), BF16)] * 4,
        compiler_params=pltpu.CompilerParams(vmem_limit_bytes=8 << 20),
        name="ingest",
    )(meta, *arrays)


def forward_step(layer, meta, blocks, gains, weights, stashes, after):
    rows, quarter = blocks[0].shape
    features = 4 * quarter
    pipe, slot, multiplies = layer % PIPES, layer // PIPES, layer < LAST

    def kernel(meta_ref, b0, b1, b2, b3, gain_ref, weight_ref, *refs):
        next_ref, hidden_ref, normed_ref, normed, total = refs[-5:]
        turn = pl.program_id(0)
        tensor = meta_ref[1]
        active = meta_ref[0] == pipe

        @pl.when(active & (turn == 0))
        def _():
            squares = 0.0
            for k, ref in enumerate((b0, b1, b2, b3)):
                hidden_ref[0, k] = ref[...]
                wide = ref[...].astype(F32)
                squares = squares + jnp.sum(wide * wide, axis=-1, keepdims=True)
            scale = lax.rsqrt(squares * (1.0 / features) + EPSILON)
            for k, ref in enumerate((b0, b1, b2, b3)):
                gain = gain_ref[slot, pl.ds(turned(tensor - k), 1), :]
                normed[k] = (ref[...].astype(F32) * scale * gain).astype(BF16)
            normed_ref[0] = normed[0]

        if multiplies:

            @pl.when(active)
            def _():
                part = jnp.dot(normed[turn], weight_ref[0], preferred_element_type=F32)

                @pl.when(turn == 0)
                def _():
                    total[...] = part

                @pl.when(turn > 0)
                def _():
                    total[...] += part

            @pl.when(active & (turn == 3))
            def _():
                rounded = total[...].astype(BF16).astype(F32)
                next_ref[...] = (b0[...].astype(F32) + rounded).astype(BF16)

    def weight_at(turn, meta_ref):
        return slot, jnp.where(meta_ref[0] == pipe, turned(meta_ref[1] - turn), 0), 0

    def stash_at(meta_ref):
        return jnp.where(meta_ref[0] == pipe, 0, 1)

    block = pl.BlockSpec((rows, quarter), lambda turn, meta_ref: (0, 0))
    return pl.pallas_call(
        kernel,
        grid_spec=pltpu.PrefetchScalarGridSpec(
            num_scalar_prefetch=1,
            grid=(4,),
            in_specs=[block] * 4
            + [
                pl.BlockSpec((2, 4, quarter), lambda turn, meta_ref: (0, 0, 0)),
                pl.BlockSpec((1, quarter, quarter), weight_at),
            ]
            + [ANYWHERE] * (len(stashes) + len(after)),
            out_specs=[
                block,
                pl.BlockSpec((1, 4, rows, quarter), lambda turn, m: (stash_at(m), 0, 0, 0)),
                pl.BlockSpec((1, rows, quarter), lambda turn, m: (stash_at(m), 0, 0)),
            ],
            scratch_shapes=[pltpu.VMEM((4, rows, quarter), BF16), pltpu.VMEM((rows, quarter), F32)],
        ),
        out_shape=[
            jax.ShapeDtypeStruct((rows, quarter), BF16),
            jax.ShapeDtypeStruct((2, 4, rows, quarter), BF16),
            jax.ShapeDtypeStruct((2, rows, quarter), BF16),
        ],
        input_output_aliases={7: 1, 8: 2} if stashes else {},
        compiler_params=pltpu.CompilerParams(vmem_limit_bytes=20 << 20),
        cost_estimate=pl.CostEstimate(
            flops=2 * rows * features * quarter, bytes_accessed=2 * features * quarter, transcendentals=0
        ),
        name="forward_step",
    )(meta, *blocks, gains, weights, *stashes, *after)


def backward_step(layer, meta, arrived, gains, weights, hidden_stash, stashes, after):
    rows, quarter = arrived[0].shape
    features = 4 * quarter
    pipe, slot, multiplies = layer % PIPES, layer // PIPES, layer > 0
    terms = len(arrived)

    def kernel(meta_ref, gain_ref, weight_ref, hidden_ref, *refs):
        own_out, o1, o2, o3, grad_ref, delta, scaled, inner = refs[-8:]
        turn = pl.program_id(0)
        tensor = meta_ref[1]
        active = meta_ref[0] == pipe

        @pl.when(active & (turn == 0))
        def _():
            total = refs[0][...].astype(F32)
            for ref in refs[1:terms]:
                total = total + ref[...].astype(F32)
            delta[...] = total.astype(BF16)
            grad_ref[0] = total.astype(BF16)

        if multiplies:

            @pl.when(active)
            def _():
                part = lax.dot_general(
                    delta[...], weight_ref[0], (((1,), (1,)), ((), ())), preferred_element_type=F32
                )
                gain = gain_ref[slot, pl.ds(turned(tensor + turn), 1), :]
                back = part.astype(BF16).astype(F32) * gain
                scaled[turn] = back
                hidden = hidden_ref[0, turned(-turn)].astype(F32)
                sums = jnp.broadcast_to(jnp.sum(hidden * back, axis=-1, keepdims=True), inner.shape)

                @pl.when(turn == 0)
                def _():
                    inner[...] = sums

                @pl.when(turn > 0)
                def _():
                    inner[...] += sums

            @pl.when(active & (turn == 3))
            def _():
                squares = 0.0
                for k in range(4):
                    wide = hidden_ref[0, k].astype(F32)
                    squares = squares + jnp.sum(wide * wide, axis=-1, keepdims=True)
                scale = lax.rsqrt(squares * (1.0 / features) + EPSILON)
                slope = scale * scale * scale * (inner[:, :1] * (1.0 / features))
                for k, ref in enumerate((own_out, o1, o2, o3)):
                    change = scale * scaled[k] - slope * hidden_ref[0, (4 - k) % 4].astype(F32)
                    if k == 0:
                        ref[...] = delta[...].astype(F32) + change
                    else:
                        ref[...] = change.astype(BF16)

    def weight_at(turn, meta_ref):
        return slot, jnp.where(meta_ref[0] == pipe, turned(meta_ref[1] + turn), 0), 0

    def stash_at(meta_ref):
        return jnp.where(meta_ref[0] == pipe, 0, 1)

    block = pl.BlockSpec((rows, quarter), lambda turn, meta_ref: (0, 0))
    return pl.pallas_call(
        kernel,
        grid_spec=pltpu.PrefetchScalarGridSpec(
            num_scalar_prefetch=1,
            grid=(4,),
            in_specs=[
                pl.BlockSpec((2, 4, quarter), lambda turn, meta_ref: (0, 0, 0)),
                pl.BlockSpec((1, quarter, quarter), weight_at),
                pl.BlockSpec((1, 4, rows, quarter), lambda turn, m: (0, 0, 0, 0)),
            ]
            + [block] * terms
            + [ANYWHERE] * (len(stashes) + len(after)),
            out_specs=[block] * 4 + [pl.BlockSpec((1, rows, quarter), lambda turn, m: (stash_at(m), 0, 0))],
            scratch_shapes=[
                pltpu.VMEM((rows, quarter), BF16),
                pltpu.VMEM((4, rows, quarter), F32),
                pltpu.VMEM((rows, 128), F32),
            ],
        ),
        out_shape=[jax.ShapeDtypeStruct((rows, quarter), F32)]
        + [jax.ShapeDtypeStruct((rows, quarter), BF16)] * 3
        + [jax.ShapeDtypeStruct((2, rows, quarter), BF16)],
        input_output_aliases={4 + terms: 4} if stashes else {},
        compiler_params=pltpu.CompilerParams(vmem_limit_bytes=20 << 20),
        cost_estimate=pl.CostEstimate(
            flops=2 * rows * features * quarter, bytes_accessed=2 * features * quarter, transcendentals=0
        ),
        name="backward_step",
    )(meta, gains, weights, hidden_stash, *arrived, *stashes, *after)


def joined(first, second, after):
    rows, columns = first.shape

    def kernel(a_ref, b_ref, *refs):
        refs[-1][:rows, :] = a_ref[...]
        refs[-1][rows:, :] = b_ref[...]

    whole = pl.BlockSpec(memory_space=pltpu.VMEM)
    return pl.pallas_call(
        kernel,
        in_specs=[whole] * 2 + [ANYWHERE] * len(after),
        out_specs=whole,
        out_shape=jax.ShapeDtypeStruct((2 * rows, columns), first.dtype),
        compiler_params=pltpu.CompilerParams(vmem_limit_bytes=8 << 20),
        name="joined",
    )(first, second, *after)


def own_columns(meta, pieces, own, after):
    rows = pieces[0].shape[0]

    def kernel(meta_ref, *refs):
        column = pl.multiple_of(meta_ref[2] * own, own)
        for k, piece in enumerate(refs[: len(pieces)]):
            refs[-1][k * rows : (k + 1) * rows, :] = piece[:, pl.ds(column, own)]

    whole = pl.BlockSpec(memory_space=pltpu.VMEM)
    return pl.pallas_call(
        kernel,
        in_specs=[pl.BlockSpec(memory_space=pltpu.SMEM)] + [whole] * len(pieces) + [ANYWHERE] * len(after),
        out_specs=whole,
        out_shape=jax.ShapeDtypeStruct((rows * len(pieces), own), BF16),
        compiler_params=pltpu.CompilerParams(vmem_limit_bytes=8 << 20),
        name="own_columns",
    )(meta, *pieces, *after)


def gram(pieces, picked, inv_tokens, after):
    quarter = pieces[0].shape[-1]
    count, own = picked[0].shape
    starts = [0]
    for piece in pieces:
        starts.append(starts[-1] + piece.shape[0])

    def kernel(*refs):
        token_refs, picked_refs, outs = refs[: len(pieces)], refs[len(pieces) : len(pieces) + 4], refs[-4:]
        for left, out in zip(picked_refs, outs):
            product = 0.0
            for ref, start, stop in zip(token_refs, starts, starts[1:]):
                product = product + lax.dot_general(
                    left[start:stop, :], ref[...], (((0,), (0,)), ((), ())), preferred_element_type=F32
                )
            out[...] = (product * inv_tokens).astype(BF16)

    whole = pl.BlockSpec(memory_space=pltpu.VMEM)
    return pl.pallas_call(
        kernel,
        in_specs=[whole] * (len(pieces) + 4) + [ANYWHERE] * len(after),
        out_specs=[whole] * 4,
        out_shape=[jax.ShapeDtypeStruct((own, quarter), BF16)] * 4,
        compiler_params=pltpu.CompilerParams(vmem_limit_bytes=20 << 20),
        cost_estimate=pl.CostEstimate(
            flops=2 * count * 4 * own * quarter,
            bytes_accessed=2 * (count * quarter + 8 * own * quarter),
            transcendentals=0,
        ),
        name="gram",
    )(*pieces, *picked, *after)


def shifted(array, x=0, y=0, z=0):
    return permuted(array, lambda p, t, u, v: (p, (t + x) % SIZES[1], u ^ z, (v + y) % SIZES[3]))


def share_columns(blocks):
    return [blocks[0]] + [shifted(blocks[4 - k], x=k) for k in (1, 2, 3)]


def assemble(meta, first, second, after):
    own, quarter = first[0].shape

    def kernel(meta_ref, *refs):
        out = refs[-1]
        tensor = meta_ref[1]
        for step in range(4):
            column = pl.multiple_of(turned(tensor - step) * quarter, quarter)
            out[:, :, pl.ds(column, quarter)] = jnp.stack([refs[step][...], refs[4 + step][...]], 1)

    whole = pl.BlockSpec(memory_space=pltpu.VMEM)
    return pl.pallas_call(
        kernel,
        in_specs=[pl.BlockSpec(memory_space=pltpu.SMEM)] + [whole] * 8 + [ANYWHERE] * len(after),
        out_specs=whole,
        out_shape=jax.ShapeDtypeStruct((own, 2, 4 * quarter), BF16),
        compiler_params=pltpu.CompilerParams(vmem_limit_bytes=20 << 20),
        name="assemble",
    )(meta, *first, *second, *after)


def body(inputs, weights, norm_gains, cotangent):
    micro_count, shard_rows, features = inputs.shape
    quarter = weights.shape[3]
    pipe = lax.axis_index("pipe")
    tensor = lax.axis_index("tensor")
    group = lax.axis_index(DP)
    own_rows = quarter // lax.axis_size(DP)
    inv_tokens = 1.0 / (micro_count * shard_rows * lax.axis_size(TENSOR_DP))
    meta = jnp.stack([pipe, tensor, group]).astype(jnp.int32)
    gains = norm_gains.reshape(norm_gains.shape[0], 4, quarter)
    weights = held(weights.reshape(weights.shape[0], features, quarter), (meta, gains))
    weights = pltpu.with_memory_space_constraint(weights, pltpu.VMEM)

    given = jnp.where(pipe == LAST % PIPES, cotangent, inputs).reshape(-1, features)
    received = ingest(meta, [given] + [shifted(given, x=k) for k in (1, 2, 3)])
    back = [shifted(received[0], z=1)]

    def over_y(rows, other, after):
        both = joined(rows, other, after)
        return [both] + [shifted(both, y=k) for k in (1, 2, 3)]

    def over_x(mine):
        return [mine] + [shifted(mine, x=k) for k in (1, 2, 3)]

    def blocks_of(pieces, picked, after):
        return share_columns(gram(pieces, picked, inv_tokens, after))

    hidden, normed, grads = {}, {}, {}
    rows, other, pieces, blocks = {}, {}, {}, {}
    due = {tick: [] for tick in range(2 * LAST + 4)}
    due[2] += back
    over_z_at = {3: "act_0", 9: "act_1", 11: "grad_1"}
    over_y_at = {4: "act_0"}
    for tick in range(2 * LAST + 1):
        waits = due[tick]
        if tick <= LAST:
            slot = tick // PIPES
            stashes = [hidden[slot], normed[slot]] if slot in hidden else []
            following, hidden[slot], normed[slot] = forward_step(
                tick, meta, received, gains, weights, stashes, waits
            )
            if tick < LAST:
                received = fan_out([following] * 4, forward_moves(tick))
                arrived = received[:1]
        if tick >= LAST:
            layer = 2 * LAST - tick
            slot = layer // PIPES
            stashes = [grads[slot]] if slot in grads else []
            *sent, grads[slot] = backward_step(
                layer, meta, back, gains, weights, hidden[slot], stashes, waits
            )
            if layer:
                back = fan_out(sent, backward_moves(layer))
                arrived = back[:1]
        if tick in over_z_at:
            name = over_z_at[tick]
            rows[name] = {"act_0": normed, "act_1": normed, "grad_1": grads}[name][int(name[-1])][0]
            other[name] = shifted(rows[name], z=1)
            due[tick + 1] += [other[name]]
        if tick in over_y_at:
            name = over_y_at[tick]
            pieces[name] = over_y(rows[name], other[name], arrived)
            for later, piece in enumerate(pieces[name][1:]):
                due[tick + 1 + later].append(piece)
    rows["grad_0"] = grads[0][0]
    other["grad_0"] = shifted(rows["grad_0"], z=1)
    for name in ("act_1", "grad_1", "grad_0"):
        pieces[name] = over_y(rows[name], other[name], [rows["grad_0"]])
    for name in ("act_0", "act_1", "grad_1", "grad_0"):
        picked = over_x(own_columns(meta, pieces[name], own_rows, [rows["grad_0"]]))
        blocks[name] = blocks_of(pieces[name], picked, [])
    act_factor = assemble(meta, blocks["act_0"], blocks["act_1"], [])
    grad_factor = assemble(meta, blocks["grad_0"], blocks["grad_1"], [])
    shape = (own_rows, 2, 1, features)
    return (act_factor.reshape(shape), grad_factor.reshape(shape))


def solution(mesh):
    split = Mesh(mesh.devices.reshape(SIZES), AXES)
    placed = (
        P(None, TENSOR_DP, None),
        P(None, "pipe", None, "tensor"),
        P(None, "pipe", None),
        P(None, TENSOR_DP, None),
    )
    return jax.shard_map(
        body,
        mesh=split,
        in_specs=placed,
        out_specs=(P(TENSOR_DP, None, "pipe", None), P(TENSOR_DP, None, "pipe", None)),
        check_vma=False,
    )
```
